32 devices in a mesh: groups: 2 (over y), expert: 8 (over z, core), hidden: 2 (over x), tok: 1.
Axes of the slice: x: 2, y: 2, z: 4, core: 2. Of those that a mesh axis runs over, the one named last changes fastest.
Arguments:
- out_grad: bfloat16 [2560, 1152], P(('groups', 'expert', 'tok')), parts along dimension 0, may hold values from -2.5 to 2.5
- expert_index: int32 [2560, 2], P(('groups', 'expert', 'tok')), parts along dimension 0, may hold values from 0 to 3, all different within a row; in each aligned block of 160 rows (0 to 159, 160 to 319, ...) at most 100 rows name the same one
- gate_values: float32 [2560, 2], P(('groups', 'expert', 'tok')), parts along dimension 0, may hold values from 0.2 to 1
- dispatched_inputs: bfloat16 [8, 800, 1152], P('expert', ('groups', 'tok')), parts along dimension 1, may hold values from -6 to 6
- w_gate: bfloat16 [8, 1152, 2304], P('expert', None, 'hidden'), may hold values from -0.1875 to 0.1875
- w_up: bfloat16 [8, 1152, 2304], P('expert', None, 'hidden'), may hold values from -0.1875 to 0.1875
- w_down: bfloat16 [8, 2304, 1152], P('expert', 'hidden'), may hold values from -0.09375 to 0.09375
Outputs:
- input_grad: bfloat16 [2560, 1152], P(('groups', 'expert', 'tok'), 'hidden'), parts along dimension 0
- gate_grad: bfloat16 [2560, 2], P(('groups', 'expert', 'tok')), parts along dimension 0
The draws below stay inside these ranges and needn't reach their ends.
There are 2 independent parts, one for each index of `groups`. The reference program is written for one: setup_inputs(seed, part) draws one part's arguments, and reference() takes and returns one part's arrays. A program takes and returns all parts, laid end to end along the dimension named above; an argument that names none is the same for every part. Nothing has to cross between parts.
Inputs may be any that keep to these rules, and one draw needn't show every extreme that they name: `expert_index`: each row names two different experts. In each aligned block of 160 rows (the rows of one device) no expert is named by more than 100 rows, and in some block some expert is named by exactly 100 rows.
All inputs are finite; a program needn't handle non-finite values.
Results may differ from the reference program's by a relative error of at most 0.014.
Values may be sent and summed in bfloat16 or wider, within the bound.
No kernel may reach another device: no remote copies, remote signals or barrier semaphores. Data moves between devices by JAX's collectives and lax.ppermute only.
A program may use at most 64 MiB of HBM per device.

```python
import math
import jax
import jax.numpy as jnp
import numpy as np
from jax import lax

D = 1152
FF = 4608
SPLIT = 2
EXPERTS = 4
TOK_DEV = 160
CAP = 100
TOKENS = 1280
N_EXPERT = 8
N_HIDDEN = 2
N_TOK = 1


def levels(key, extent, pieces, low, high):
    loudness, own = 1.0, jax.random.fold_in(key, 6)
    for position, blocks in pieces:
        heights = jnp.exp(jax.random.uniform(jax.random.fold_in(own, position), (blocks,), jnp.float32, low / len(pieces), high / len(pieces)))
        loudness = loudness * jnp.repeat(heights, extent[position] // blocks).reshape([-1 if axis == position else 1 for axis in range(len(extent))])
    return loudness


def shared_out(own_key, own, number, rows, number_of, top, limit, lean):
    ranking = jax.random.permutation(own_key, number_of)
    heavy_load, common = load_shares(number_of, rows * top, limit, lean, True), load_shares(number_of, rows * top, limit, lean, False)
    places = jnp.arange(number_of)

    def named(tallies, turn):
        used = int((tallies > 0).sum())
        fixed = max(1, used // 4)
        moved = fixed + (places - fixed + turn * (used - fixed)) % max(1, number_of - fixed)
        return jnp.zeros((number_of,), jnp.int32).at[ranking[jnp.where(places < fixed, places, moved)]].set(jnp.asarray(tallies, jnp.int32))

    tallies = jnp.where(number % 4 == 0, named(heavy_load, number // 4), named(common, number - number // 4 - 1))
    mixed = jax.random.permutation(jax.random.fold_in(own, 3), number_of)
    source_of, receiver = mixed[0:number_of // 2 * 2:2], mixed[1:number_of // 2 * 2:2]
    room = jnp.minimum(tallies[source_of] - 1, limit - tallies[receiver]) // 2
    room = jnp.where((source_of == ranking[0]) | (receiver == ranking[0]) | (tallies[receiver] == 0), 0, jnp.maximum(room, 0))
    moved = jax.random.randint(jax.random.fold_in(own, 4), (number_of // 2,), 0, 1 << 20) % (room + 1)
    tallies = tallies.at[source_of].add(-moved).at[receiver].add(moved)
    members = jnp.searchsorted(jnp.cumsum(tallies), jnp.arange(rows * top), side="right").astype(jnp.int32)
    grid = members.reshape(top, rows).T
    grid = grid[jax.random.permutation(jax.random.fold_in(own, 1), rows)]
    turn = jax.random.randint(jax.random.fold_in(own, 2), (rows, 1), 0, top)
    return jnp.take_along_axis(grid, (jnp.arange(top)[None, :] + turn) % top, axis=1)


def load_shares(amount, total, limit, skew, full):
    portions = [(1 << 20) // math.isqrt(standing ** skew) + 1 for standing in range(1, amount + 1)]
    largest = limit if full else min(limit, max(-(-total // amount), total * portions[0] // sum(portions)))
    least = 1 if total - largest >= amount - 1 else 0
    holding, spare = [largest] + [least] * (amount - 1), total - largest - least * (amount - 1)
    while spare > 0:
        candidates = [i for i in range(1, amount) if holding[i] < largest] or [i for i in range(1, amount) if holding[i] < limit]
        pool, budget = sum([portions[i] for i in candidates]), spare
        for i in candidates:
            addition = min(limit - holding[i], max(1, budget * portions[i] // pool), spare)
            holding[i] = holding[i] + addition
            spare = spare - addition
    return np.array(holding)


def bell_draw(own_key, shape, width, reach, split=(), kind=jnp.bfloat16):
    entries = jax.random.normal(own_key, shape, jnp.float32) * width
    if len(split) > 0:
        entries = levels(own_key, shape, split, -0.22, 0.18) * entries
    return jnp.clip(entries, min=-reach, max=reach).astype(kind)


def setup_inputs(seed: int = 0, part: int = 0) -> dict:
    key_list = jax.random.split(jax.random.key(seed), 8)
    part_splits = jax.random.split(jax.random.fold_in(key_list[7], part), 8)
    out_grad = bell_draw(part_splits[0], (TOKENS, D), 0.25, 2.5, ((0, 8),))
    expert_index_keys = jax.random.split(jax.random.fold_in(part_splits[1], 1), TOKENS // TOK_DEV)
    expert_index_turns = jax.random.permutation(jax.random.fold_in(part_splits[1], 3), TOKENS // TOK_DEV)
    expert_index = jax.vmap(lambda own, number: shared_out(jax.random.fold_in(part_splits[1], 2), own, number, TOK_DEV, EXPERTS, 2, CAP, 2))(expert_index_keys, expert_index_turns).reshape((TOKENS, 2))
    gate_values = jnp.clip(0.2 + 0.8 * jax.random.uniform(part_splits[2], (TOKENS, 2), jnp.float32) ** levels(part_splits[2], (TOKENS, 2), ((0, 8),), -0.2, 0.2), 0.2, 1.0)
    dispatched_inputs = bell_draw(part_splits[3], (N_EXPERT, N_TOK * N_EXPERT * CAP // SPLIT, D), 1.0, 6.0, ((0, 8),))
    w_gate = bell_draw(key_list[4], (N_EXPERT, D, FF // SPLIT), D ** -0.5, 0.1875, ((0, 8), (2, 2)))
    w_up = bell_draw(key_list[5], (N_EXPERT, D, FF // SPLIT), D ** -0.5, 0.1875, ((0, 8), (2, 2)))
    w_down = bell_draw(key_list[6], (N_EXPERT, FF // SPLIT, D), FF ** -0.5, 0.09375, ((0, 8), (1, 2)))
    return dict(out_grad=out_grad, expert_index=expert_index, gate_values=gate_values, dispatched_inputs=dispatched_inputs, w_gate=w_gate, w_up=w_up, w_down=w_down)


def slots_of(index_block):
    flat_expert = index_block.reshape(-1)
    onehot = (flat_expert[:, None] == jnp.arange(EXPERTS, dtype=jnp.int32)[None, :]).astype(jnp.int32)
    before = jnp.cumsum(onehot, axis=0) - onehot
    return jnp.sum(onehot * before, axis=1).astype(jnp.int32)


def one_expert(operands):
    inputs, cotangent, gate_mat, up_mat, down_mat = operands
    slot_count = inputs.shape[0]
    group_total = SPLIT * N_HIDDEN
    group_units = FF // group_total
    gate_pre = jnp.dot(inputs, gate_mat, preferred_element_type=jnp.float32)
    up_pre = jnp.dot(inputs, up_mat, preferred_element_type=jnp.float32)
    sigmoid_gate = jax.nn.sigmoid(gate_pre)
    hidden_act = gate_pre * sigmoid_gate * up_pre
    d_hidden = jnp.dot(cotangent, down_mat.T, preferred_element_type=jnp.float32)
    d_up = (d_hidden * gate_pre * sigmoid_gate).astype(jnp.bfloat16)
    d_gate = (d_hidden * up_pre * sigmoid_gate * (1.0 + gate_pre * (1.0 - sigmoid_gate))).astype(jnp.bfloat16)
    gate_terms = jnp.sum((hidden_act * d_hidden).reshape(slot_count, group_total, group_units), axis=2)
    gate_terms = lax.optimization_barrier(gate_terms.astype(jnp.bfloat16)).astype(jnp.float32)
    slot_gate = jnp.sum(gate_terms, axis=1).astype(jnp.bfloat16)
    back_terms = jnp.einsum("rhf,dhf->hrd",
                            d_gate.astype(jnp.float32).reshape(slot_count, group_total, group_units),
                            gate_mat.astype(jnp.float32).reshape(D, group_total, group_units),
                            precision=lax.Precision.HIGHEST)
    back_terms = back_terms + jnp.einsum("rhf,dhf->hrd",
                                         d_up.astype(jnp.float32).reshape(slot_count, group_total, group_units),
                                         up_mat.astype(jnp.float32).reshape(D, group_total, group_units),
                                         precision=lax.Precision.HIGHEST)
    back_terms = lax.optimization_barrier(back_terms.astype(jnp.bfloat16)).astype(jnp.float32)
    slot_grad = jnp.sum(back_terms, axis=0).astype(jnp.bfloat16)
    return slot_grad, slot_gate


def reference(out_grad, expert_index, gate_values, dispatched_inputs, w_gate, w_up, w_down):
    shard_total = N_EXPERT * N_TOK
    slot_total = N_TOK * N_EXPERT * CAP
    half_rows = N_EXPERT * CAP // SPLIT
    half_units = FF // SPLIT
    gate_full = w_gate.reshape(EXPERTS, SPLIT, D, half_units).transpose(0, 2, 1, 3).reshape(EXPERTS, D, FF)
    up_full = w_up.reshape(EXPERTS, SPLIT, D, half_units).transpose(0, 2, 1, 3).reshape(EXPERTS, D, FF)
    down_full = w_down.reshape(EXPERTS, FF, D)
    expert_inputs = dispatched_inputs.reshape(EXPERTS, SPLIT, N_TOK, half_rows, D)
    expert_inputs = expert_inputs.transpose(0, 2, 1, 3, 4).reshape(EXPERTS, slot_total, D)
    slot = jax.vmap(slots_of)(expert_index.reshape(shard_total, TOK_DEV, 2)).reshape(TOKENS, 2)
    shard_id = jnp.arange(TOKENS, dtype=jnp.int32) // TOK_DEV
    source_id = shard_id // N_TOK
    tok_id = shard_id % N_TOK
    dest_row = (expert_index * slot_total + tok_id[:, None] * (N_EXPERT * CAP)
                + source_id[:, None] * CAP + slot).astype(jnp.int32)
    flat_dest = dest_row.reshape(-1)
    routed_grad = jnp.zeros((EXPERTS * slot_total, D), jnp.bfloat16)
    routed_grad = routed_grad.at[flat_dest].set(jnp.repeat(out_grad, 2, axis=0))
    routed_grad = routed_grad.reshape(EXPERTS, slot_total, D)
    slot_grad, slot_gate = lax.map(one_expert, (expert_inputs, routed_grad, gate_full, up_full, down_full))
    picked = slot_grad.reshape(EXPERTS * slot_total, D)[flat_dest].astype(jnp.float32).reshape(TOKENS, 2, D)
    input_grad = jnp.sum(gate_values[:, :, None] * picked, axis=1).astype(jnp.bfloat16)
    gate_grad = slot_gate.reshape(-1)[flat_dest].reshape(TOKENS, 2)
    return input_grad, gate_grad
```

```python
import functools

import jax
import jax.numpy as jnp
from jax import lax
from jax.experimental import pallas as pl
from jax.experimental.pallas import tpu as pltpu
from jax.sharding import PartitionSpec as P

LANES = 128
NT = (((1,), (1,)), ((), ()))
TN = (((0,), (0,)), ((), ()))
VMEM_LIMIT = 40 << 20


def params():
    return pltpu.CompilerParams(vmem_limit_bytes=VMEM_LIMIT)


def whole():
    return pl.BlockSpec(memory_space=pltpu.VMEM)


def smem():
    return pl.BlockSpec(memory_space=pltpu.SMEM)


def dot(a, b, dims=(((1,), (0,)), ((), ()))):
    return lax.dot_general(a, b, dims, preferred_element_type=jnp.float32)


def relative(expert_index, peer, peers):
    shifted = expert_index - peer
    return jnp.where(shifted < 0, shifted + peers, shifted)


def named_by(rel, rows):
    lane = lax.broadcasted_iota(jnp.int32, (rows, LANES), 1)
    return (rel[:, 0:1] == lane) | (rel[:, 1:2] == lane)


def route_kernel(peers, padded, meta, index_ref, grad_ref, *outs):
    rows = grad_ref.shape[0]
    rel = relative(index_ref[...], meta[0], peers)
    named = named_by(rel, rows).astype(jnp.bfloat16)
    first = lax.broadcasted_iota(jnp.int32, (rows, rows), 0)
    second = lax.broadcasted_iota(jnp.int32, (rows, rows), 1)
    slots = dot(named, (first < second).astype(jnp.bfloat16), TN)
    present = dot(named, (first == second).astype(jnp.bfloat16), TN)
    place = lax.broadcasted_iota(jnp.int32, (padded, rows), 0)
    grad = grad_ref[...]
    for d, out in enumerate(outs):
        pick = (place == slots[d : d + 1, :].astype(jnp.int32)) & (present[d : d + 1, :] > 0.5)
        out[...] = dot(pick.astype(jnp.bfloat16), grad).astype(jnp.bfloat16)


def route(meta, expert_index, out_grad, peers, padded):
    rows, width = out_grad.shape
    return pl.pallas_call(
        functools.partial(route_kernel, peers, padded),
        out_shape=[jax.ShapeDtypeStruct((padded, width), jnp.bfloat16)] * peers,
        in_specs=[smem(), whole(), whole()],
        out_specs=[whole()] * peers,
        compiler_params=params(),
        cost_estimate=pl.CostEstimate(
            flops=2 * peers * padded * rows * width,
            bytes_accessed=2 * width * (rows + peers * padded),
            transcendentals=0,
        ),
        name="route",
    )(meta, expert_index, out_grad)


def forward_kernel(peers, cap, padded, order, meta, own_ref, other_ref, gate_ref, up_ref, act_ref, slope_ref, hid_ref, own32, other32, rows_ref):
    half_rows = own_ref.shape[0]

    @pl.when(pl.program_id(0) == 0)
    def _():
        for source, wide in ((own_ref, own32), (other_ref, other32)):
            wide[pl.ds(0, half_rows), :] = source[...].astype(jnp.float32)
            wide[pl.ds(half_rows, wide.shape[0] - half_rows), :] = jnp.zeros(
                (wide.shape[0] - half_rows, wide.shape[1]), jnp.float32
            )
        peer, pair = meta[0], meta[1]
        for wide, half in ((own32, pair), (other32, 1 - pair)):
            for k in range(peers):
                source = half * peers + k
                away = peer - lax.div(source, 2)
                away = jnp.where(away < 0, away + peers, away)
                swap = jnp.where(lax.rem(source, 2) == pair, 0, 1)
                position = 0
                for n, (d, core) in enumerate(order):
                    position += jnp.where((away == d) & (swap == core), n, 0)
                target = pl.ds(pl.multiple_of(position * padded, 16), padded)
                rows_ref[target, :] = wide[pl.ds(k * cap, padded), :].astype(jnp.bfloat16)

    rows = rows_ref[...]
    gate = dot(rows, gate_ref[0])
    up = dot(rows, up_ref[0])
    sig = jax.nn.sigmoid(gate)
    act = gate * sig
    act_ref[...] = act.astype(jnp.bfloat16)
    slope_ref[...] = (up * sig * (1.0 + gate * (1.0 - sig))).astype(jnp.bfloat16)
    hid_ref[...] = (act * up).astype(jnp.bfloat16)


def unit_block(units):
    for size in (384, 256, 128):
        if units % size == 0:
            return size
    return units


def forward(meta, own, other, w_gate, w_up, peers, cap, padded, order):
    half_rows, width = own.shape
    units = w_gate.shape[2]
    block = unit_block(units)
    rows = len(order) * padded
    deep = -(-(half_rows + padded) // 16) * 16
    column = pl.BlockSpec((rows, block), lambda j: (0, j))
    weight = pl.BlockSpec((1, width, block), lambda j: (0, 0, j))
    return pl.pallas_call(
        functools.partial(forward_kernel, peers, cap, padded, order),
        grid=(units // block,),
        out_shape=[jax.ShapeDtypeStruct((rows, units), jnp.bfloat16)] * 3,
        in_specs=[smem(), whole(), whole(), weight, weight],
        out_specs=[column] * 3,
        scratch_shapes=[
            pltpu.VMEM((deep, width), jnp.float32),
            pltpu.VMEM((deep, width), jnp.float32),
            pltpu.VMEM((rows, width), jnp.bfloat16),
        ],
        compiler_params=params(),
        cost_estimate=pl.CostEstimate(
            flops=4 * rows * width * units,
            bytes_accessed=2 * (2 * width * units + 3 * rows * units + rows * width),
            transcendentals=rows * units,
        ),
        name="forward",
    )(meta, own, other, w_gate, w_up)


def backward_kernel(count, cap, padded, meta, *refs):
    cots = refs[:count]
    act_ref, slope_ref, hid_ref, gate_ref, up_ref, down_ref = refs[count : count + 6]
    keep, give, cot_ref, sum_ref, part_ref = refs[count + 6 :]
    step = pl.program_id(0)

    @pl.when(step == 0)
    def _():
        for n, cot in enumerate(cots):
            cot_ref[pl.ds(n * padded, padded), :] = cot[...]

    d_hidden = dot(cot_ref[...], down_ref[0], NT)
    part = jnp.sum(d_hidden * hid_ref[...].astype(jnp.float32), axis=1, keepdims=True)
    d_gate = (d_hidden * slope_ref[...].astype(jnp.float32)).astype(jnp.bfloat16)
    d_up = (d_hidden * act_ref[...].astype(jnp.float32)).astype(jnp.bfloat16)
    back = dot(d_gate, gate_ref[0], NT) + dot(d_up, up_ref[0], NT)

    @pl.when(step == 0)
    def _():
        sum_ref[...] = back
        part_ref[...] = jnp.broadcast_to(part, part_ref.shape)

    @pl.when(step > 0)
    def _():
        sum_ref[...] += back
        part_ref[...] += jnp.broadcast_to(part, part_ref.shape)

    @pl.when(step == pl.num_programs(0) - 1)
    def _():
        shares, kept, share = give.shape
        row = lax.broadcasted_iota(jnp.int32, (padded, share), 0)
        lane = lax.broadcasted_iota(jnp.int32, (padded, LANES), 1)
        diagonal = lax.broadcasted_iota(jnp.int32, (padded, LANES), 0) == lane
        for n in range(count):
            rows = pl.ds(n * padded, padded)
            total = sum_ref[rows, :]
            line = jnp.sum(jnp.where(diagonal, part_ref[rows, :], 0.0), axis=0, keepdims=True)
            line = jnp.concatenate([line, jnp.zeros((1, share - LANES), jnp.float32)], axis=1)
            pieces = [total[:, i * share : (i + 1) * share] for i in range(shares)]
            for r in range(shares):
                piece = pieces[r]
                for i in range(shares):
                    piece = jnp.where(meta[2] == (i - r) % shares, pieces[i], piece)
                piece = jnp.where(row < cap, piece, jnp.where(row == cap, line, 0.0))
                if n < count // 2:
                    keep[r, rows, :] = piece
                else:
                    give[r, pl.ds(n * padded - kept, padded), :] = piece.astype(jnp.bfloat16)


def backward(meta, cots, first, tables, w_gate, w_up, w_down, cap, padded, shares):
    count = len(cots)
    width = cots[0].shape[1]
    units = w_gate.shape[2]
    block = unit_block(units)
    rows = count * padded
    kept = rows // 2
    share = width // shares
    table = pl.BlockSpec((rows, block), lambda j: (first, j))
    weight = pl.BlockSpec((1, width, block), lambda j: (0, 0, j))
    return pl.pallas_call(
        functools.partial(backward_kernel, count, cap, padded),
        grid=(units // block,),
        out_shape=[
            jax.ShapeDtypeStruct((shares, kept, share), jnp.float32),
            jax.ShapeDtypeStruct((shares, kept, share), jnp.bfloat16),
        ],
        in_specs=[smem()]
        + [whole()] * count
        + [table] * 3
        + [weight, weight, pl.BlockSpec((1, block, width), lambda j: (0, j, 0))],
        out_specs=[whole()] * 2,
        scratch_shapes=[
            pltpu.VMEM((rows, width), jnp.bfloat16),
            pltpu.VMEM((rows, width), jnp.float32),
            pltpu.VMEM((rows, LANES), jnp.float32),
        ],
        compiler_params=params(),
        cost_estimate=pl.CostEstimate(
            flops=6 * rows * width * units,
            bytes_accessed=2 * (3 * width * units + 3 * rows * units + 4 * rows * width),
            transcendentals=0,
        ),
        name="backward",
    )(meta, *cots, *tables, w_gate, w_up, w_down)


def combine_kernel(peers, cap, meta, index_ref, gates_ref, *refs):
    blocks = refs[:peers]
    grad_ref, gate_out = refs[peers:]
    rows = index_ref.shape[0]
    padded = blocks[0].shape[0]
    rel = relative(index_ref[...], meta[0], peers)
    gates = gates_ref[...]
    named = named_by(rel, rows)
    first = lax.broadcasted_iota(jnp.int32, (rows, rows), 0)
    second = lax.broadcasted_iota(jnp.int32, (rows, rows), 1)
    slots = dot((second < first).astype(jnp.bfloat16), named.astype(jnp.bfloat16)).astype(jnp.int32)
    place = lax.broadcasted_iota(jnp.int32, (rows, padded), 1)
    total = jnp.zeros(grad_ref.shape, jnp.float32)
    products = jnp.zeros((rows, 2), jnp.float32)
    for d, block in enumerate(blocks):
        chosen = rel == d
        weight = jnp.sum(jnp.where(chosen, gates, 0.0), axis=1, keepdims=True)
        hit = jnp.max(chosen.astype(jnp.int32), axis=1, keepdims=True) > 0
        pick = (place == slots[:, d : d + 1]) & hit
        values = block[...]
        total += weight * dot(pick.astype(jnp.bfloat16), values)
        line = values[cap : cap + 1, :padded].astype(jnp.float32)
        found = jnp.sum(jnp.where(pick, line, 0.0), axis=1, keepdims=True)
        products += jnp.where(chosen, found, 0.0)
    grad_ref[...] = total.astype(jnp.bfloat16)
    gate_out[...] = products.astype(jnp.bfloat16)


def combine(meta, expert_index, gate_values, blocks, cap):
    rows = expert_index.shape[0]
    peers = len(blocks)
    padded, share = blocks[0].shape
    return pl.pallas_call(
        functools.partial(combine_kernel, peers, cap),
        out_shape=[
            jax.ShapeDtypeStruct((rows, share), jnp.bfloat16),
            jax.ShapeDtypeStruct((rows, 2), jnp.bfloat16),
        ],
        in_specs=[smem()] + [whole()] * (2 + peers),
        out_specs=[whole()] * 2,
        compiler_params=params(),
        cost_estimate=pl.CostEstimate(
            flops=2 * peers * padded * rows * share,
            bytes_accessed=2 * share * (rows + peers * padded),
            transcendentals=0,
        ),
        name="combine",
    )(meta, expert_index, gate_values, *blocks)


def swap_pair(block):
    count = lax.axis_size("expert")
    return lax.ppermute(block, "expert", [(i, i ^ 1) for i in range(count)])


def sum_hidden(pieces):
    count = lax.axis_size("hidden")
    total = pieces[0]
    for r in range(1, count):
        ring = [(i, (i + r) % count) for i in range(count)]
        total = total + lax.ppermute(pieces[r].astype(jnp.bfloat16), "hidden", ring).astype(jnp.float32)
    return total.astype(jnp.bfloat16)


def shifted(block, d):
    count = lax.axis_size("expert")
    return lax.ppermute(block, "expert", [(i, (i + 2 * d) % count) for i in range(count)])


def local(out_grad, expert_index, gate_values, dispatched_inputs, w_gate, w_up, w_down):
    peers = lax.axis_size("expert") // 2
    shares = lax.axis_size("hidden")
    index = lax.axis_index("expert")
    meta = jnp.stack([index // 2, index % 2, lax.axis_index("hidden")]).astype(jnp.int32)
    own_rows = dispatched_inputs[0]
    cap = own_rows.shape[0] // peers
    padded = (cap // 16 + 1) * 16
    other_rows = swap_pair(own_rows)
    sent = route(meta, expert_index, out_grad, peers, padded)

    far = sorted(range(1, peers), key=lambda d: -min(d, peers - d))
    arrived = {0: sent[0]}
    for d in far:
        arrived[d] = shifted(sent[d], d)
    ranked = [0] + far
    groups = [ranked[: peers // 2], ranked[peers // 2 :]]
    order = []
    for group in groups:
        order += [(d, 0) for d in group] + [(d, 1) for d in group]
    tables = forward(meta, own_rows, other_rows, w_gate, w_up, peers, cap, padded, tuple(order))

    returned = {}
    for n, group in enumerate(groups):
        cots = [arrived[d] for d in group] + [swap_pair(arrived[d]) for d in group]
        keep, give = backward(
            meta, cots, n, tables, w_gate, w_up, w_down, cap, padded, shares
        )
        got = swap_pair(give)
        total = sum_hidden([keep[r] + got[r].astype(jnp.float32) for r in range(shares)])
        for m, d in enumerate(group):
            block = total[m * padded : (m + 1) * padded]
            returned[d] = shifted(block, -d) if d else block
    blocks = [returned[d] for d in range(peers)]
    return tuple(combine(meta, expert_index, gate_values, blocks, cap))


def solution(mesh):
    in_specs = (
        P(("groups", "expert", "tok"), None),
        P(("groups", "expert", "tok"), None),
        P(("groups", "expert", "tok"), None),
        P("expert", ("groups", "tok"), None),
        P("expert", None, "hidden"),
        P("expert", None, "hidden"),
        P("expert", "hidden", None),
    )
    out_specs = (P(("groups", "expert", "tok"), "hidden"), P(("groups", "expert", "tok"), None))
    return jax.shard_map(local, mesh=mesh, in_specs=in_specs, out_specs=out_specs, check_vma=False)
```

```python
import functools

import jax
import jax.numpy as jnp
from jax import lax
from jax.experimental import pallas as pl
from jax.experimental.pallas import tpu as pltpu
from jax.sharding import PartitionSpec as P

LANES = 128
NT = (((1,), (1,)), ((), ()))


def params(limit=10 << 20):
    return pltpu.CompilerParams(vmem_limit_bytes=limit)


def whole():
    return pl.BlockSpec(memory_space=pltpu.VMEM)


def smem():
    return pl.BlockSpec(memory_space=pltpu.SMEM)


def cost():
    return pl.CostEstimate(flops=1000, bytes_accessed=1000, transcendentals=0)


def in_hbm(value):
    return pltpu.with_memory_space_constraint(value, pltpu.HBM)


def dot(a, b, dims=(((1,), (0,)), ((), ()))):
    return lax.dot_general(a, b, dims, preferred_element_type=jnp.float32)


def ring(value, peers):
    return jnp.where(value < 0, value + peers, value)


def named_rows(index_ref, peer, peers):
    rel = ring(index_ref[...] - peer, peers)
    count, rows = rel.shape
    expert = lax.broadcasted_iota(jnp.int32, (-(-peers // 8) * 8, rows), 0)
    named = rel[0:1, :] == expert
    for k in range(1, count):
        named = named | (rel[k : k + 1, :] == expert)
    return rel, named


def slot_rows(named):
    rows = named.shape[1]
    first = lax.broadcasted_iota(jnp.int32, (rows, rows), 0)
    second = lax.broadcasted_iota(jnp.int32, (rows, rows), 1)
    before = dot(named.astype(jnp.bfloat16), (first < second).astype(jnp.bfloat16))
    return jnp.where(named, before.astype(jnp.int32), -1)


def route_kernel(peers, padded, spread, meta, index_hbm, grad_hbm, *refs):
    outs, (index_ref, grad_ref, sems) = refs[:peers], refs[peers:]
    copies = [
        pltpu.make_async_copy(index_hbm, index_ref, sems.at[0]),
        pltpu.make_async_copy(grad_hbm, grad_ref, sems.at[1]),
    ]
    for copy in copies:
        copy.start()
    copies[0].wait()
    rows = grad_ref.shape[0]
    _, named = named_rows(index_ref, meta[0], peers)
    slots = slot_rows(named)
    place = lax.broadcasted_iota(jnp.int32, (padded, rows), 0)
    copies[1].wait()
    grad = grad_ref[...]
    for d, out in enumerate(outs):
        pick = (place == slots[d : d + 1, :]).astype(jnp.bfloat16)
        block = dot(pick, grad)
        share = out.shape[1]
        if d in spread:
            chosen = block[:, :share]
            for i in range(1, block.shape[1] // share):
                chosen = jnp.where(meta[2] == i, block[:, i * share : (i + 1) * share], chosen)
            block = chosen
        out[...] = block.astype(jnp.bfloat16)


def route(meta, index_rows, out_grad, peers, padded, spread, shares):
    width = out_grad.shape[1]
    hbm = pl.BlockSpec(memory_space=pltpu.HBM)
    return pl.pallas_call(
        functools.partial(route_kernel, peers, padded, spread),
        out_shape=[
            jax.ShapeDtypeStruct((padded, width // shares if d in spread else width), jnp.bfloat16)
            for d in range(peers)
        ],
        in_specs=[smem(), hbm, hbm],
        out_specs=[whole()] * peers,
        scratch_shapes=[
            pltpu.VMEM(index_rows.shape, index_rows.dtype),
            pltpu.VMEM(out_grad.shape, out_grad.dtype),
            pltpu.SemaphoreType.DMA((2,)),
        ],
        compiler_params=params(),
        cost_estimate=cost(),
        name="route",
    )(meta, in_hbm(index_rows), in_hbm(out_grad))


def unit_blocks(units):
    return [pl.ds(start, min(256, units - start)) for start in range(0, units, 256)]


def forward_kernel(peers, cap, padded, order, meta, own_hbm, other_ref, gate_hbm, up_hbm, down_hbm, act_ref, slope_ref, hid_ref, gate_ref, up_ref, down_ref, own_ref, rows_ref, sems):
    first = pltpu.make_async_copy(own_hbm.at[0], own_ref, sems.at[0])
    last = pltpu.make_async_copy(down_hbm.at[0], down_ref, sems.at[1])
    first.start()
    units = unit_blocks(gate_ref.shape[1])
    loads = []
    for n, unit in enumerate(units):
        loads.append(
            [
                pltpu.make_async_copy(source.at[0, :, unit], target.at[:, unit], sems.at[2 + 2 * n + m])
                for m, (source, target) in enumerate(((gate_hbm, gate_ref), (up_hbm, up_ref)))
            ]
        )
        for load in loads[-1]:
            load.start()
    last.start()
    peer, pair = meta[0], meta[1]
    first.wait()
    for values, half in ((own_ref[...], pair), (other_ref[...], 1 - pair)):
        for k in range(peers):
            source = half * peers + k
            away = ring(peer - lax.div(source, 2), peers)
            swap = jnp.where(lax.rem(source, 2) == pair, 0, 1)
            position = 0
            for n, (d, core) in enumerate(order):
                position += jnp.where((away == d) & (swap == core), n, 0)
            target = pl.ds(pl.multiple_of(position * padded, 16), padded)
            block = values[k * cap : (k + 1) * cap]
            empty = jnp.zeros((padded - cap, values.shape[1]), values.dtype)
            rows_ref[target, :] = jnp.concatenate([block, empty], axis=0)
    rows = rows_ref[...]
    for unit, load in zip(units, loads):
        for copy in load:
            copy.wait()
        gate = dot(rows, gate_ref[:, unit])
        up = dot(rows, up_ref[:, unit])
        sig = jax.nn.sigmoid(gate)
        act = gate * sig
        act_ref[:, unit] = act.astype(jnp.bfloat16)
        slope_ref[:, unit] = (up * (sig + act * (1.0 - sig))).astype(jnp.bfloat16)
        hid_ref[:, unit] = (act * up).astype(jnp.bfloat16)
    last.wait()


def forward(meta, dispatched, other, w_gate, w_up, w_down, peers, cap, padded, order):
    half_rows, width = other.shape
    units = w_gate.shape[2]
    rows = len(order) * padded
    hbm = pl.BlockSpec(memory_space=pltpu.HBM)
    weights = [w_gate, w_up, w_down]
    return pl.pallas_call(
        functools.partial(forward_kernel, peers, cap, padded, order),
        out_shape=[jax.ShapeDtypeStruct((rows, units), jnp.bfloat16)] * 3
        + [pltpu.VMEM(w.shape[1:], w.dtype) for w in weights],
        in_specs=[smem(), hbm, whole(), hbm, hbm, hbm],
        out_specs=[whole()] * 6,
        scratch_shapes=[
            pltpu.VMEM((half_rows, width), jnp.bfloat16),
            pltpu.VMEM((rows, width), jnp.bfloat16),
            pltpu.SemaphoreType.DMA((2 + 2 * len(unit_blocks(units)),)),
        ],
        compiler_params=params(14 << 20),
        cost_estimate=cost(),
        name="forward",
    )(meta, in_hbm(dispatched), other, *[in_hbm(w) for w in weights])


def backward_kernel(counts, cap, first, meta, *refs):
    cots, refs = refs[: sum(counts)], refs[sum(counts) :]
    act_ref, slope_ref, hid_ref, gate_ref, up_ref, down_ref, keep, give, cot_ref, gate_grad, up_grad = refs
    padded = cots[0].shape[0]
    at = 0
    for n, parts in enumerate(counts):
        pieces = [ref[...] for ref in cots[at : at + parts]]
        at += parts
        full = jnp.concatenate([pieces[-i % parts] for i in range(parts)], axis=1)
        for h in range(1, parts):
            turned = jnp.concatenate([pieces[(h - i) % parts] for i in range(parts)], axis=1)
            full = jnp.where(meta[2] == h, turned, full)
        cot_ref[pl.ds(n * padded, padded), :] = full
    rows = pl.ds(first, len(counts) * padded)
    cot = cot_ref[...]
    part = jnp.zeros((len(counts) * padded, 1), jnp.float32)
    for unit in unit_blocks(gate_ref.shape[1]):
        d_hidden = dot(cot, down_ref[unit, :], NT)
        part += jnp.sum(d_hidden * hid_ref[rows, unit].astype(jnp.float32), axis=1, keepdims=True)
        gate_grad[:, unit] = (d_hidden * slope_ref[rows, unit].astype(jnp.float32)).astype(jnp.bfloat16)
        up_grad[:, unit] = (d_hidden * act_ref[rows, unit].astype(jnp.float32)).astype(jnp.bfloat16)
    back = dot(gate_grad[...], gate_ref[...], NT) + dot(up_grad[...], up_ref[...], NT)
    shares, kept, share = give.shape
    row = lax.broadcasted_iota(jnp.int32, (padded, share), 0)
    lane = lax.broadcasted_iota(jnp.int32, (padded, LANES), 1)
    diagonal = lax.broadcasted_iota(jnp.int32, (padded, LANES), 0) == lane
    for n in range(len(counts)):
        block = slice(n * padded, (n + 1) * padded)
        out, start = (keep, n * padded) if n < len(counts) // 2 else (give, n * padded - kept)
        line = jnp.sum(jnp.where(diagonal, part[block], 0.0), axis=0, keepdims=True)
        line = jnp.concatenate([line, jnp.zeros((1, share - LANES), jnp.float32)], axis=1)
        pieces = [back[block, i * share : (i + 1) * share] for i in range(shares)]
        for r in range(shares):
            piece = pieces[r]
            for i in range(shares):
                if i != r:
                    piece = jnp.where(meta[2] == (i - r) % shares, pieces[i], piece)
            piece = jnp.where(row < cap, piece, jnp.where(row == cap, line, 0.0))
            out[r, pl.ds(start, padded), :] = piece.astype(out.dtype)


def backward(meta, cots, tables, first, gate_mat, up_mat, down_mat, cap, shares):
    padded = cots[0][0].shape[0]
    width, units = gate_mat.shape
    rows = len(cots) * padded
    share = width // shares
    parts = [part for cot in cots for part in cot]
    return pl.pallas_call(
        functools.partial(backward_kernel, [len(cot) for cot in cots], cap, first),
        out_shape=[
            jax.ShapeDtypeStruct((shares, rows // 2, share), jnp.float32),
            jax.ShapeDtypeStruct((shares, rows // 2, share), jnp.bfloat16),
        ],
        in_specs=[smem()] + [whole()] * (len(parts) + 6),
        out_specs=[whole()] * 2,
        scratch_shapes=[
            pltpu.VMEM((rows, width), jnp.bfloat16),
            pltpu.VMEM((rows, units), jnp.bfloat16),
            pltpu.VMEM((rows, units), jnp.bfloat16),
        ],
        compiler_params=params(14 << 20),
        cost_estimate=cost(),
        name="backward",
    )(meta, *parts, *tables, gate_mat, up_mat, down_mat)


def combine_kernel(peers, cap, meta, index_ref, gates_ref, *refs):
    blocks = refs[:peers]
    grad_ref, gate_out = refs[peers:]
    rows = grad_ref.shape[0]
    padded = blocks[0].shape[0]
    rel, named = named_rows(index_ref, meta[0], peers)
    slots = slot_rows(named)
    gates = gates_ref[...]
    diagonal = lax.broadcasted_iota(jnp.int32, (rows, rows), 0) == lax.broadcasted_iota(
        jnp.int32, (rows, rows), 1
    )

    def column(row):
        return jnp.sum(jnp.where(diagonal, row, 0), axis=1, keepdims=True)

    place = lax.broadcasted_iota(jnp.int32, (rows, padded), 1)
    total = jnp.zeros(grad_ref.shape, jnp.float32)
    products = jnp.zeros(rel.shape, jnp.float32)
    for d, block in enumerate(blocks):
        chosen = rel == d
        weight = column(jnp.sum(jnp.where(chosen, gates, 0.0), axis=0, keepdims=True))
        pick = (place == column(slots[d : d + 1, :])).astype(jnp.bfloat16)
        values = block[...]
        total += weight * dot(pick, values)
        found = dot(values[cap:padded, :padded], pick, NT)
        products += jnp.where(chosen, found[0:1, :], 0.0)
    grad_ref[...] = total.astype(jnp.bfloat16)
    gate_out[...] = products.astype(jnp.bfloat16)


def combine(meta, index_rows, gate_rows, blocks, cap):
    count, rows = index_rows.shape
    peers = len(blocks)
    padded, share = blocks[0].shape
    return pl.pallas_call(
        functools.partial(combine_kernel, peers, cap),
        out_shape=[
            jax.ShapeDtypeStruct((rows, share), jnp.bfloat16),
            jax.ShapeDtypeStruct((count, rows), jnp.bfloat16),
        ],
        in_specs=[smem()] + [whole()] * (2 + peers),
        out_specs=[whole()] * 2,
        compiler_params=params(),
        cost_estimate=cost(),
        name="combine",
    )(meta, index_rows, gate_rows, *blocks)


def after(value, others):
    return lax.optimization_barrier((value, others))[0]


def swap_pair(block):
    count = lax.axis_size("expert")
    return lax.ppermute(block, "expert", [(i, i ^ 1) for i in range(count)])


def hidden_ring(block, r):
    count = lax.axis_size("hidden")
    return lax.ppermute(block, "hidden", [(i, (i + r) % count) for i in range(count)])


def shifted(block, d):
    count = lax.axis_size("expert")
    return lax.ppermute(block, "expert", [(i, (i + 2 * d) % count) for i in range(count)])


def chunk_groups(peers):
    rest = sorted(range(1, peers), key=lambda d: (-min(d, peers - d), d))
    rest = rest[:1] + sorted(rest[1:], key=lambda d: (min(d, peers - d), d))
    return [[0]] + [rest[n : n + 2] for n in range(0, len(rest), 2)]


def local(out_grad, expert_index, gate_values, dispatched_inputs, w_gate, w_up, w_down):
    peers = lax.axis_size("expert") // 2
    shares = lax.axis_size("hidden")
    index = lax.axis_index("expert")
    meta = jnp.stack([index // 2, index % 2, lax.axis_index("hidden")]).astype(jnp.int32)
    half_rows = dispatched_inputs.shape[1]
    cap = half_rows // peers
    padded = (cap // 16 + 1) * 16
    index_rows = expert_index.T
    other_rows = swap_pair(dispatched_inputs[0])
    sent = route(meta, index_rows, out_grad, peers, padded, (), shares)
    arrived = [shifted(block, d) if d else block for d, block in enumerate(sent)]

    groups = chunk_groups(peers)
    order = tuple((d, swap) for group in groups for swap in (0, 1) for d in group)
    *tables, gate_mat, up_mat, down_mat = forward(
        meta, dispatched_inputs, other_rows, w_gate, w_up, w_down, peers, cap, padded, order
    )

    gives, crossings, totals, returned = [], [], [], {}
    first = 0
    ready = {d: arrived[d] for d in groups[0]}

    def finish(n, later):
        total, parts, _ = crossings[n]
        for part in after(parts, later):
            total = total + part.astype(jnp.float32)
        totals.append(total.astype(jnp.bfloat16))
        for m, d in enumerate(groups[n]):
            block = totals[n][m * padded : (m + 1) * padded]
            returned[d] = shifted(block, -d) if d else block

    for n, group in enumerate(groups):
        swapped = {d: swap_pair(ready[d]) for d in group}
        cots = [[ready[d]] for d in group] + [[swapped[d]] for d in group]
        cots = after(cots, ([c[2] for c in crossings], totals, gives))
        keep, give = backward(meta, cots, tables, first, gate_mat, up_mat, down_mat, cap, shares)
        first += 2 * len(group) * padded
        gives.append(give)
        ready = {}
        for d in groups[n + 1] if n + 1 < len(groups) else []:
            ready[d] = after(arrived[d], give)
        done = list(ready.values())
        if n:
            finish(n - 1, give)
            done.append(totals[-1])
        got = swap_pair(after(give, done))
        pieces = [keep[r] + got[r].astype(jnp.float32) for r in range(shares)]
        crossing = [piece.astype(jnp.bfloat16) for piece in pieces[1:]]
        crossings.append((pieces[0], [hidden_ring(c, r + 1) for r, c in enumerate(crossing)], crossing))
    finish(len(groups) - 1, [])
    blocks = [returned[d] for d in range(peers)]
    input_grad, gate_grad = combine(meta, index_rows, gate_values.T, blocks, cap)
    return input_grad, gate_grad.T


def solution(mesh):
    in_specs = (
        P(("groups", "expert", "tok"), None),
        P(("groups", "expert", "tok"), None),
        P(("groups", "expert", "tok"), None),
        P("expert", ("groups", "tok"), None),
        P("expert", None, "hidden"),
        P("expert", None, "hidden"),
        P("expert", "hidden", None),
    )
    out_specs = (P(("groups", "expert", "tok"), "hidden"), P(("groups", "expert", "tok"), None))
    return jax.shard_map(local, mesh=mesh, in_specs=in_specs, out_specs=out_specs, check_vma=False)
```

```python
import functools

import jax
import jax.numpy as jnp
from jax import lax
from jax.experimental import pallas as pl
from jax.experimental.pallas import tpu as pltpu
from jax.sharding import PartitionSpec as P

LANES = 128
NT = (((1,), (1,)), ((), ()))


def params(limit=10 << 20):
    return pltpu.CompilerParams(vmem_limit_bytes=limit)


def whole():
    return pl.BlockSpec(memory_space=pltpu.VMEM)


def smem():
    return pl.BlockSpec(memory_space=pltpu.SMEM)


def cost():
    return pl.CostEstimate(flops=1000, bytes_accessed=1000, transcendentals=0)


def in_hbm(value):
    return pltpu.with_memory_space_constraint(value, pltpu.HBM)


def dot(a, b, dims=(((1,), (0,)), ((), ()))):
    return lax.dot_general(a, b, dims, preferred_element_type=jnp.float32)


def ring(value, peers):
    return jnp.where(value < 0, value + peers, value)


def named_rows(index_ref, peer, peers):
    rel = ring(index_ref[...] - peer, peers)
    count, rows = rel.shape
    expert = lax.broadcasted_iota(jnp.int32, (-(-peers // 8) * 8, rows), 0)
    named = rel[0:1, :] == expert
    for k in range(1, count):
        named = named | (rel[k : k + 1, :] == expert)
    return rel, named


def slot_rows(named):
    rows = named.shape[1]
    first = lax.broadcasted_iota(jnp.int32, (rows, rows), 0)
    second = lax.broadcasted_iota(jnp.int32, (rows, rows), 1)
    before = dot(named.astype(jnp.bfloat16), (first < second).astype(jnp.bfloat16))
    return jnp.where(named, before.astype(jnp.int32), -1)


def route_kernel(peers, padded, spread, meta, index_hbm, grad_hbm, *refs):
    outs, (index_ref, grad_ref, sems) = refs[:peers], refs[peers:]
    copies = [
        pltpu.make_async_copy(index_hbm, index_ref, sems.at[0]),
        pltpu.make_async_copy(grad_hbm, grad_ref, sems.at[1]),
    ]
    for copy in copies:
        copy.start()
    copies[0].wait()
    rows = grad_ref.shape[0]
    _, named = named_rows(index_ref, meta[0], peers)
    slots = slot_rows(named)
    place = lax.broadcasted_iota(jnp.int32, (padded, rows), 0)
    copies[1].wait()
    grad = grad_ref[...]
    for d, out in enumerate(outs):
        pick = (place == slots[d : d + 1, :]).astype(jnp.bfloat16)
        block = dot(pick, grad)
        share = out.shape[1]
        if d in spread:
            chosen = block[:, :share]
            for i in range(1, block.shape[1] // share):
                chosen = jnp.where(meta[2] == i, block[:, i * share : (i + 1) * share], chosen)
            block = chosen
        out[...] = block.astype(jnp.bfloat16)


def route(meta, index_rows, out_grad, peers, padded, spread, shares):
    width = out_grad.shape[1]
    hbm = pl.BlockSpec(memory_space=pltpu.HBM)
    return pl.pallas_call(
        functools.partial(route_kernel, peers, padded, spread),
        out_shape=[
            jax.ShapeDtypeStruct((padded, width // shares if d in spread else width), jnp.bfloat16)
            for d in range(peers)
        ],
        in_specs=[smem(), hbm, hbm],
        out_specs=[whole()] * peers,
        scratch_shapes=[
            pltpu.VMEM(index_rows.shape, index_rows.dtype),
            pltpu.VMEM(out_grad.shape, out_grad.dtype),
            pltpu.SemaphoreType.DMA((2,)),
        ],
        compiler_params=params(),
        cost_estimate=cost(),
        name="route",
    )(meta, in_hbm(index_rows), in_hbm(out_grad))


def unit_blocks(units):
    return [pl.ds(start, min(256, units - start)) for start in range(0, units, 256)]


def forward_kernel(peers, cap, padded, order, meta, own_hbm, other_ref, gate_hbm, up_hbm, down_hbm, act_ref, slope_ref, hid_ref, gate_ref, up_ref, down_ref, own_ref, rows_ref, sems):
    first = pltpu.make_async_copy(own_hbm.at[0], own_ref, sems.at[0])
    last = pltpu.make_async_copy(down_hbm.at[0], down_ref, sems.at[1])
    first.start()
    units = unit_blocks(gate_ref.shape[1])
    loads = []
    for n, unit in enumerate(units):
        loads.append(
            [
                pltpu.make_async_copy(source.at[0, :, unit], target.at[:, unit], sems.at[2 + 2 * n + m])
                for m, (source, target) in enumerate(((gate_hbm, gate_ref), (up_hbm, up_ref)))
            ]
        )
        for load in loads[-1]:
            load.start()
    last.start()
    peer, pair = meta[0], meta[1]
    first.wait()
    for values, half in ((own_ref[...], pair), (other_ref[...], 1 - pair)):
        for k in range(peers):
            source = half * peers + k
            away = ring(peer - lax.div(source, 2), peers)
            swap = jnp.where(lax.rem(source, 2) == pair, 0, 1)
            position = 0
            for n, (d, core) in enumerate(order):
                position += jnp.where((away == d) & (swap == core), n, 0)
            target = pl.ds(pl.multiple_of(position * padded, 16), padded)
            block = values[k * cap : (k + 1) * cap]
            empty = jnp.zeros((padded - cap, values.shape[1]), values.dtype)
            rows_ref[target, :] = jnp.concatenate([block, empty], axis=0)
    rows = rows_ref[...]
    for unit, load in zip(units, loads):
        for copy in load:
            copy.wait()
        gate = dot(rows, gate_ref[:, unit])
        up = dot(rows, up_ref[:, unit])
        sig = jax.nn.sigmoid(gate)
        act = gate * sig
        act_ref[:, unit] = act.astype(jnp.bfloat16)
        slope_ref[:, unit] = (up * (sig + act * (1.0 - sig))).astype(jnp.bfloat16)
        hid_ref[:, unit] = (act * up).astype(jnp.bfloat16)
    last.wait()


def forward(meta, dispatched, other, w_gate, w_up, w_down, peers, cap, padded, order):
    half_rows, width = other.shape
    units = w_gate.shape[2]
    rows = len(order) * padded
    hbm = pl.BlockSpec(memory_space=pltpu.HBM)
    weights = [w_gate, w_up, w_down]
    return pl.pallas_call(
        functools.partial(forward_kernel, peers, cap, padded, order),
        out_shape=[jax.ShapeDtypeStruct((rows, units), jnp.bfloat16)] * 3
        + [pltpu.VMEM(w.shape[1:], w.dtype) for w in weights],
        in_specs=[smem(), hbm, whole(), hbm, hbm, hbm],
        out_specs=[whole()] * 6,
        scratch_shapes=[
            pltpu.VMEM((half_rows, width), jnp.bfloat16),
            pltpu.VMEM((rows, width), jnp.bfloat16),
            pltpu.SemaphoreType.DMA((2 + 2 * len(unit_blocks(units)),)),
        ],
        compiler_params=params(14 << 20),
        cost_estimate=cost(),
        name="forward",
    )(meta, in_hbm(dispatched), other, *[in_hbm(w) for w in weights])


def backward_kernel(counts, cap, padded, first, meta, *refs):
    cots, refs = refs[: sum(counts)], refs[sum(counts) :]
    act_ref, slope_ref, hid_ref, gate_ref, up_ref, down_ref, keep = refs[:7]
    gives, (cot_ref, gate_grad, up_grad) = refs[7:-3], refs[-3:]
    sent_rows = cots[0].shape[0]
    at = 0
    for n, parts in enumerate(counts):
        pieces = [ref[...] for ref in cots[at : at + parts]]
        at += parts
        full = jnp.concatenate([pieces[-i % parts] for i in range(parts)], axis=1)
        for h in range(1, parts):
            turned = jnp.concatenate([pieces[(h - i) % parts] for i in range(parts)], axis=1)
            full = jnp.where(meta[2] == h, turned, full)
        if padded > sent_rows:
            empty = jnp.zeros((padded - sent_rows, full.shape[1]), full.dtype)
            full = jnp.concatenate([full, empty], axis=0)
        cot_ref[pl.ds(n * padded, padded), :] = full
    rows = pl.ds(first, len(counts) * padded)
    cot = cot_ref[...]
    part = jnp.zeros((len(counts) * padded, 1), jnp.float32)
    for unit in unit_blocks(gate_ref.shape[1]):
        d_hidden = dot(cot, down_ref[unit, :], NT)
        part += jnp.sum(d_hidden * hid_ref[rows, unit].astype(jnp.float32), axis=1, keepdims=True)
        gate_grad[:, unit] = (d_hidden * slope_ref[rows, unit].astype(jnp.float32)).astype(jnp.bfloat16)
        up_grad[:, unit] = (d_hidden * act_ref[rows, unit].astype(jnp.float32)).astype(jnp.bfloat16)
    back = dot(gate_grad[...], gate_ref[...], NT) + dot(up_grad[...], up_ref[...], NT)
    shares, _, share = keep.shape
    row = lax.broadcasted_iota(jnp.int32, (sent_rows, share), 0)
    lane = lax.broadcasted_iota(jnp.int32, (sent_rows, LANES), 1)
    diagonal = lax.broadcasted_iota(jnp.int32, (sent_rows, LANES), 0) == lane
    blocks = [[] for _ in range(shares)]
    for n in range(len(counts)):
        block = slice(n * padded, n * padded + sent_rows)
        line = jnp.sum(jnp.where(diagonal, part[block], 0.0), axis=0, keepdims=True)
        line = jnp.concatenate([line, jnp.zeros((1, share - LANES), jnp.float32)], axis=1)
        pieces = [back[block, i * share : (i + 1) * share] for i in range(shares)]
        for r in range(shares):
            piece = pieces[r]
            for i in range(shares):
                if i != r:
                    piece = jnp.where(meta[2] == (i - r) % shares, pieces[i], piece)
            blocks[r].append(jnp.where(row < cap, piece, jnp.where(row == cap, line, 0.0)))
    half = len(counts) // 2
    for r in range(shares):
        keep[r] = jnp.concatenate(blocks[r][:half], axis=0)
        gives[r][...] = jnp.concatenate(blocks[r][half:], axis=0).astype(jnp.bfloat16)


def backward(meta, cots, tables, first, gate_mat, up_mat, down_mat, cap, padded, shares):
    kept = len(cots) // 2 * cots[0][0].shape[0]
    width, units = gate_mat.shape
    rows = len(cots) * padded
    share = width // shares
    parts = [part for cot in cots for part in cot]
    return pl.pallas_call(
        functools.partial(backward_kernel, [len(cot) for cot in cots], cap, padded, first),
        out_shape=[
            jax.ShapeDtypeStruct((shares, kept, share), jnp.float32),
            *[jax.ShapeDtypeStruct((kept, share), jnp.bfloat16)] * shares,
        ],
        in_specs=[smem()] + [whole()] * (len(parts) + 6),
        out_specs=[whole()] * (1 + shares),
        scratch_shapes=[
            pltpu.VMEM((rows, width), jnp.bfloat16),
            pltpu.VMEM((rows, units), jnp.bfloat16),
            pltpu.VMEM((rows, units), jnp.bfloat16),
        ],
        compiler_params=params(14 << 20),
        cost_estimate=cost(),
        name="backward",
    )(meta, *parts, *tables, gate_mat, up_mat, down_mat)


def combine_kernel(peers, cap, early, late, meta, index_ref, gates_ref, *refs):
    blocks = refs[: len(early)]
    sum_ref, product_ref, pick_ref, weight_ref = refs[len(early) :]
    rows, padded = sum_ref.shape[0], pick_ref.shape[2]
    rel, named = named_rows(index_ref, meta[0], peers)
    slots = slot_rows(named)
    gates = gates_ref[...]
    diagonal = lax.broadcasted_iota(jnp.int32, (rows, rows), 0) == lax.broadcasted_iota(
        jnp.int32, (rows, rows), 1
    )

    def column(row):
        return jnp.sum(jnp.where(diagonal, row, 0), axis=1, keepdims=True)

    place = lax.broadcasted_iota(jnp.int32, (rows, padded), 1)
    total = jnp.zeros(sum_ref.shape, jnp.float32)
    products = jnp.zeros(rel.shape, jnp.float32)
    for n, d in enumerate(early + late):
        chosen = rel == d
        weight = column(jnp.sum(jnp.where(chosen, gates, 0.0), axis=0, keepdims=True))
        pick = (place == column(slots[d : d + 1, :])).astype(jnp.bfloat16)
        if n < len(early):
            values = blocks[n][...]
            total += weight * dot(pick, values)
            found = dot(values[cap:padded, :padded], pick, NT)
            products += jnp.where(chosen, found[0:1, :], 0.0)
        else:
            pick_ref[n - len(early)] = pick
            weight_ref[n - len(early)] = jnp.broadcast_to(weight, weight_ref.shape[1:])
    sum_ref[...] = total
    product_ref[...] = products


def combine_late_kernel(peers, cap, late, meta, index_ref, sum_in, product_in, pick_ref, weight_ref, *refs):
    blocks, (grad_ref, gate_out) = refs[: len(late)], refs[len(late) :]
    rel = ring(index_ref[...] - meta[0], peers)
    total = sum_in[...]
    products = product_in[...]
    for n, (d, block) in enumerate(zip(late, blocks)):
        values, pick = block[...], pick_ref[n]
        padded = values.shape[0]
        total += weight_ref[n][:, 0:1] * dot(pick, values)
        found = dot(values[cap:padded, :padded], pick, NT)
        products += jnp.where(rel == d, found[0:1, :], 0.0)
    grad_ref[...] = total.astype(jnp.bfloat16)
    gate_out[...] = products.astype(jnp.bfloat16)


def combine(meta, index_rows, gate_rows, returned, early, late, cap):
    count, rows = index_rows.shape
    peers = len(early) + len(late)
    padded, share = returned[0].shape
    partial = pl.pallas_call(
        functools.partial(combine_kernel, peers, cap, early, late),
        out_shape=[
            jax.ShapeDtypeStruct((rows, share), jnp.float32),
            jax.ShapeDtypeStruct((count, rows), jnp.float32),
            jax.ShapeDtypeStruct((len(late), rows, padded), jnp.bfloat16),
            jax.ShapeDtypeStruct((len(late), rows, LANES), jnp.float32),
        ],
        in_specs=[smem()] + [whole()] * (2 + len(early)),
        out_specs=[whole()] * 4,
        compiler_params=params(),
        cost_estimate=cost(),
        name="combine",
    )(meta, index_rows, gate_rows, *[returned[d] for d in early])
    return pl.pallas_call(
        functools.partial(combine_late_kernel, peers, cap, late),
        out_shape=[
            jax.ShapeDtypeStruct((rows, share), jnp.bfloat16),
            jax.ShapeDtypeStruct((count, rows), jnp.bfloat16),
        ],
        in_specs=[smem()] + [whole()] * (5 + len(late)),
        out_specs=[whole()] * 2,
        compiler_params=params(),
        cost_estimate=cost(),
        name="combine_late",
    )(meta, index_rows, *partial, *[returned[d] for d in late])


def after(value, others):
    return lax.optimization_barrier((value, others))[0]


def swap_pair(block):
    count = lax.axis_size("expert")
    return lax.ppermute(block, "expert", [(i, i ^ 1) for i in range(count)])


def hidden_ring(block, r):
    count = lax.axis_size("hidden")
    return lax.ppermute(block, "hidden", [(i, (i + r) % count) for i in range(count)])


def shifted(block, d):
    count = lax.axis_size("expert")
    return lax.ppermute(block, "expert", [(i, (i + 2 * d) % count) for i in range(count)])


def chunk_groups(peers):
    rest = sorted(range(1, peers), key=lambda d: (-min(d, peers - d), d))
    rest = rest[:1] + sorted(rest[1:], key=lambda d: (min(d, peers - d), d))
    return [[0]] + [rest[n : n + 2] for n in range(0, len(rest), 2)]


def local(out_grad, expert_index, gate_values, dispatched_inputs, w_gate, w_up, w_down):
    peers = lax.axis_size("expert") // 2
    shares = lax.axis_size("hidden")
    index = lax.axis_index("expert")
    meta = jnp.stack([index // 2, index % 2, lax.axis_index("hidden")]).astype(jnp.int32)
    half_rows = dispatched_inputs.shape[1]
    cap = half_rows // peers
    sent_rows = (cap // 8 + 1) * 8
    padded = -(-sent_rows // 16) * 16
    index_rows = expert_index.T
    other_rows = swap_pair(dispatched_inputs[0])
    sent = route(meta, index_rows, out_grad, peers, sent_rows, (), shares)
    arrived = [shifted(block, d) if d else block for d, block in enumerate(sent)]

    groups = chunk_groups(peers)
    order = tuple((d, swap) for group in groups for swap in (0, 1) for d in group)
    *tables, gate_mat, up_mat, down_mat = forward(
        meta, dispatched_inputs, other_rows, w_gate, w_up, w_down, peers, cap, padded, order
    )

    gives, crossings, totals, returned = [], [], [], {}
    first = 0
    ready = {d: arrived[d] for d in groups[0]}

    def finish(n, later):
        total, parts, _ = crossings[n]
        for part in after(parts, later):
            total = total + part.astype(jnp.float32)
        totals.append(total.astype(jnp.bfloat16))
        for m, d in enumerate(groups[n]):
            block = totals[n][m * sent_rows : (m + 1) * sent_rows]
            returned[d] = shifted(block, -d) if d else block

    for n, group in enumerate(groups):
        swapped = {d: swap_pair(ready[d]) for d in group}
        cots = [[ready[d]] for d in group] + [[swapped[d]] for d in group]
        cots = after(cots, ([c[2] for c in crossings], totals, gives))
        keep, *give = backward(
            meta, cots, tables, first, gate_mat, up_mat, down_mat, cap, padded, shares
        )
        first += 2 * len(group) * padded
        gives.append(give)
        ready = {}
        for d in groups[n + 1] if n + 1 < len(groups) else []:
            ready[d] = after(arrived[d], give)
        done = list(ready.values())
        if n:
            finish(n - 1, give)
            done.append(totals[-1])
        got = after([swap_pair(part) for part in give], done)
        pieces = [keep[r] + got[r].astype(jnp.float32) for r in range(shares)]
        crossing = [piece.astype(jnp.bfloat16) for piece in pieces[1:]]
        crossings.append((pieces[0], [hidden_ring(c, r + 1) for r, c in enumerate(crossing)], crossing))
    finish(len(groups) - 1, [])
    late = sorted({d for d in groups[1][:1] + groups[-1] if d})
    early = [d for d in range(peers) if d not in late]
    input_grad, gate_grad = combine(
        meta, index_rows, gate_values.T, returned, early, late, cap
    )
    return input_grad, gate_grad.T


def solution(mesh):
    in_specs = (
        P(("groups", "expert", "tok"), None),
        P(("groups", "expert", "tok"), None),
        P(("groups", "expert", "tok"), None),
        P("expert", ("groups", "tok"), None),
        P("expert", None, "hidden"),
        P("expert", None, "hidden"),
        P("expert", "hidden", None),
    )
    out_specs = (P(("groups", "expert", "tok"), "hidden"), P(("groups", "expert", "tok"), None))
    return jax.shard_map(local, mesh=mesh, in_specs=in_specs, out_specs=out_specs, check_vma=False)
```

```python
import functools

import jax
import jax.numpy as jnp
from jax import lax
from jax.experimental import pallas as pl
from jax.experimental.pallas import tpu as pltpu
from jax.sharding import PartitionSpec as P

LANES = 128
NT = (((1,), (1,)), ((), ()))


def params(limit=10 << 20):
    return pltpu.CompilerParams(vmem_limit_bytes=limit)


def whole():
    return pl.BlockSpec(memory_space=pltpu.VMEM)


def smem():
    return pl.BlockSpec(memory_space=pltpu.SMEM)


def cost():
    return pl.CostEstimate(flops=1000, bytes_accessed=1000, transcendentals=0)


def in_hbm(value):
    return pltpu.with_memory_space_constraint(value, pltpu.HBM)


def dot(a, b, dims=(((1,), (0,)), ((), ()))):
    return lax.dot_general(a, b, dims, preferred_element_type=jnp.float32)


def ring(value, peers):
    return jnp.where(value < 0, value + peers, value)


def named_rows(index_ref, peer, peers):
    rel = ring(index_ref[...] - peer, peers)
    count, rows = rel.shape
    expert = lax.broadcasted_iota(jnp.int32, (-(-peers // 8) * 8, rows), 0)
    named = rel[0:1, :] == expert
    for k in range(1, count):
        named = named | (rel[k : k + 1, :] == expert)
    return rel, named


def slot_rows(named):
    rows = named.shape[1]
    first = lax.broadcasted_iota(jnp.int32, (rows, rows), 0)
    second = lax.broadcasted_iota(jnp.int32, (rows, rows), 1)
    before = dot(named.astype(jnp.bfloat16), (first < second).astype(jnp.bfloat16))
    return jnp.where(named, before.astype(jnp.int32), -1)


def route_kernel(peers, padded, spread, meta, index_hbm, grad_hbm, *refs):
    outs, (index_ref, grad_ref, sems) = refs[:peers], refs[peers:]
    copies = [
        pltpu.make_async_copy(index_hbm, index_ref, sems.at[0]),
        pltpu.make_async_copy(grad_hbm, grad_ref, sems.at[1]),
    ]
    for copy in copies:
        copy.start()
    copies[0].wait()
    rows = grad_ref.shape[0]
    _, named = named_rows(index_ref, meta[0], peers)
    slots = slot_rows(named)
    place = lax.broadcasted_iota(jnp.int32, (padded, rows), 0)
    copies[1].wait()
    grad = grad_ref[...]
    for d, out in enumerate(outs):
        pick = (place == slots[d : d + 1, :]).astype(jnp.bfloat16)
        block = dot(pick, grad)
        share = out.shape[1]
        if d in spread:
            chosen = block[:, :share]
            for i in range(1, block.shape[1] // share):
                chosen = jnp.where(meta[2] == i, block[:, i * share : (i + 1) * share], chosen)
            block = chosen
        out[...] = block.astype(jnp.bfloat16)


def route(meta, index_rows, out_grad, peers, padded, spread, shares):
    width = out_grad.shape[1]
    hbm = pl.BlockSpec(memory_space=pltpu.HBM)
    return pl.pallas_call(
        functools.partial(route_kernel, peers, padded, spread),
        out_shape=[
            jax.ShapeDtypeStruct((padded, width // shares if d in spread else width), jnp.bfloat16)
            for d in range(peers)
        ],
        in_specs=[smem(), hbm, hbm],
        out_specs=[whole()] * peers,
        scratch_shapes=[
            pltpu.VMEM(index_rows.shape, index_rows.dtype),
            pltpu.VMEM(out_grad.shape, out_grad.dtype),
            pltpu.SemaphoreType.DMA((2,)),
        ],
        compiler_params=params(),
        cost_estimate=cost(),
        name="route",
    )(meta, in_hbm(index_rows), in_hbm(out_grad))


def unit_blocks(units):
    return [pl.ds(start, min(256, units - start)) for start in range(0, units, 256)]


def forward_kernel(peers, cap, padded, order, meta, own_hbm, other_ref, gate_hbm, up_hbm, down_hbm, act_ref, slope_ref, hid_ref, gate_ref, up_ref, down_ref, own_ref, rows_ref, sems):
    first = pltpu.make_async_copy(own_hbm.at[0], own_ref, sems.at[0])
    last = pltpu.make_async_copy(down_hbm.at[0], down_ref, sems.at[1])
    first.start()
    units = unit_blocks(gate_ref.shape[1])
    loads = []
    for n, unit in enumerate(units):
        loads.append(
            [
                pltpu.make_async_copy(source.at[0, :, unit], target.at[:, unit], sems.at[2 + 2 * n + m])
                for m, (source, target) in enumerate(((gate_hbm, gate_ref), (up_hbm, up_ref)))
            ]
        )
        for load in loads[-1]:
            load.start()
    last.start()
    peer, pair = meta[0], meta[1]
    first.wait()
    for values, half in ((own_ref[...], pair), (other_ref[...], 1 - pair)):
        for k in range(peers):
            source = half * peers + k
            away = ring(peer - lax.div(source, 2), peers)
            swap = jnp.where(lax.rem(source, 2) == pair, 0, 1)
            position = 0
            for n, (d, core) in enumerate(order):
                position += jnp.where((away == d) & (swap == core), n, 0)
            target = pl.ds(pl.multiple_of(position * padded, 16), padded)
            block = values[k * cap : (k + 1) * cap]
            empty = jnp.zeros((padded - cap, values.shape[1]), values.dtype)
            rows_ref[target, :] = jnp.concatenate([block, empty], axis=0)
    rows = rows_ref[...]
    for unit, load in zip(units, loads):
        for copy in load:
            copy.wait()
        gate = dot(rows, gate_ref[:, unit])
        up = dot(rows, up_ref[:, unit])
        sig = jax.nn.sigmoid(gate)
        act = gate * sig
        act_ref[:, unit] = act.astype(jnp.bfloat16)
        slope_ref[:, unit] = (up * (sig + act * (1.0 - sig))).astype(jnp.bfloat16)
        hid_ref[:, unit] = (act * up).astype(jnp.bfloat16)
    last.wait()


def forward(meta, dispatched, other, w_gate, w_up, w_down, peers, cap, padded, order):
    half_rows, width = other.shape
    units = w_gate.shape[2]
    rows = len(order) * padded
    hbm = pl.BlockSpec(memory_space=pltpu.HBM)
    weights = [w_gate, w_up, w_down]
    return pl.pallas_call(
        functools.partial(forward_kernel, peers, cap, padded, order),
        out_shape=[jax.ShapeDtypeStruct((rows, units), jnp.bfloat16)] * 3
        + [pltpu.VMEM(w.shape[1:], w.dtype) for w in weights],
        in_specs=[smem(), hbm, whole(), hbm, hbm, hbm],
        out_specs=[whole()] * 6,
        scratch_shapes=[
            pltpu.VMEM((half_rows, width), jnp.bfloat16),
            pltpu.VMEM((rows, width), jnp.bfloat16),
            pltpu.SemaphoreType.DMA((2 + 2 * len(unit_blocks(units)),)),
        ],
        compiler_params=params(14 << 20),
        cost_estimate=cost(),
        name="forward",
    )(meta, in_hbm(dispatched), other, *[in_hbm(w) for w in weights])


def backward_kernel(counts, cap, padded, first, meta, *refs):
    cots, refs = refs[: sum(counts)], refs[sum(counts) :]
    act_ref, slope_ref, hid_ref, gate_ref, up_ref, down_ref, keep = refs[:7]
    gives, (cot_ref, gate_grad, up_grad) = refs[7:-3], refs[-3:]
    sent_rows = cots[0].shape[0]
    at = 0
    for n, parts in enumerate(counts):
        pieces = [ref[...] for ref in cots[at : at + parts]]
        at += parts
        full = jnp.concatenate([pieces[-i % parts] for i in range(parts)], axis=1)
        for h in range(1, parts):
            turned = jnp.concatenate([pieces[(h - i) % parts] for i in range(parts)], axis=1)
            full = jnp.where(meta[2] == h, turned, full)
        if padded > sent_rows:
            empty = jnp.zeros((padded - sent_rows, full.shape[1]), full.dtype)
            full = jnp.concatenate([full, empty], axis=0)
        cot_ref[pl.ds(n * padded, padded), :] = full
    rows = pl.ds(first, len(counts) * padded)
    cot = cot_ref[...]
    part = jnp.zeros((len(counts) * padded, 1), jnp.float32)
    for unit in unit_blocks(gate_ref.shape[1]):
        d_hidden = dot(cot, down_ref[unit, :], NT)
        part += jnp.sum(d_hidden * hid_ref[rows, unit].astype(jnp.float32), axis=1, keepdims=True)
        gate_grad[:, unit] = (d_hidden * slope_ref[rows, unit].astype(jnp.float32)).astype(jnp.bfloat16)
        up_grad[:, unit] = (d_hidden * act_ref[rows, unit].astype(jnp.float32)).astype(jnp.bfloat16)
    back = dot(gate_grad[...], gate_ref[...], NT) + dot(up_grad[...], up_ref[...], NT)
    shares, _, share = keep.shape
    row = lax.broadcasted_iota(jnp.int32, (sent_rows, share), 0)
    lane = lax.broadcasted_iota(jnp.int32, (sent_rows, LANES), 1)
    diagonal = lax.broadcasted_iota(jnp.int32, (sent_rows, LANES), 0) == lane
    blocks = [[] for _ in range(shares)]
    for n in range(len(counts)):
        block = slice(n * padded, n * padded + sent_rows)
        line = jnp.sum(jnp.where(diagonal, part[block], 0.0), axis=0, keepdims=True)
        line = jnp.concatenate([line, jnp.zeros((1, share - LANES), jnp.float32)], axis=1)
        pieces = [back[block, i * share : (i + 1) * share] for i in range(shares)]
        for r in range(shares):
            piece = pieces[r]
            for i in range(shares):
                if i != r:
                    piece = jnp.where(meta[2] == (i - r) % shares, pieces[i], piece)
            blocks[r].append(jnp.where(row < cap, piece, jnp.where(row == cap, line, 0.0)))
    half = len(counts) // 2
    for r in range(shares):
        keep[r] = jnp.concatenate(blocks[r][:half], axis=0)
        gives[r][...] = jnp.concatenate(blocks[r][half:], axis=0).astype(jnp.bfloat16)


def backward(meta, cots, tables, first, gate_mat, up_mat, down_mat, cap, padded, shares):
    kept = len(cots) // 2 * cots[0][0].shape[0]
    width, units = gate_mat.shape
    rows = len(cots) * padded
    share = width // shares
    parts = [part for cot in cots for part in cot]
    return pl.pallas_call(
        functools.partial(backward_kernel, [len(cot) for cot in cots], cap, padded, first),
        out_shape=[
            jax.ShapeDtypeStruct((shares, kept, share), jnp.float32),
            *[jax.ShapeDtypeStruct((kept, share), jnp.bfloat16)] * shares,
        ],
        in_specs=[smem()] + [whole()] * (len(parts) + 6),
        out_specs=[whole()] * (1 + shares),
        scratch_shapes=[
            pltpu.VMEM((rows, width), jnp.bfloat16),
            pltpu.VMEM((rows, units), jnp.bfloat16),
            pltpu.VMEM((rows, units), jnp.bfloat16),
        ],
        compiler_params=params(14 << 20),
        cost_estimate=cost(),
        name="backward",
    )(meta, *parts, *tables, gate_mat, up_mat, down_mat)


def combine_kernel(peers, cap, early, late, meta, index_ref, gates_ref, *refs):
    blocks = refs[: len(early)]
    sum_ref, product_ref, pick_ref, weight_ref, chosen_ref = refs[len(early) :]
    rows, padded = sum_ref.shape[0], pick_ref.shape[2]
    rel, named = named_rows(index_ref, meta[0], peers)
    slots = slot_rows(named)
    gates = gates_ref[...]
    diagonal = lax.broadcasted_iota(jnp.int32, (rows, rows), 0) == lax.broadcasted_iota(
        jnp.int32, (rows, rows), 1
    )

    def column(row):
        return jnp.sum(jnp.where(diagonal, row, 0), axis=1, keepdims=True)

    place = lax.broadcasted_iota(jnp.int32, (rows, padded), 1)
    total = jnp.zeros(sum_ref.shape, jnp.float32)
    products = jnp.zeros(rel.shape, jnp.float32)
    for n, d in enumerate(early + late):
        chosen = rel == d
        weight = column(jnp.sum(jnp.where(chosen, gates, 0.0), axis=0, keepdims=True))
        pick = (place == column(slots[d : d + 1, :])).astype(jnp.bfloat16)
        if n < len(early):
            values = blocks[n][...]
            total += weight * dot(pick, values)
            found = dot(values[cap:padded, :padded], pick, NT)
            products += jnp.where(chosen, found[0:1, :], 0.0)
        else:
            pick_ref[n - len(early)] = pick
            weight_ref[n - len(early)] = jnp.broadcast_to(weight, weight_ref.shape[1:])
            chosen_ref[n - len(early)] = chosen.astype(jnp.float32)
    sum_ref[...] = total
    product_ref[...] = products


def combine_late_kernel(cap, sum_in, product_in, pick_ref, weight_ref, chosen_ref, *refs):
    blocks, (grad_ref, gate_out) = refs[:-2], refs[-2:]
    total = sum_in[...]
    products = product_in[...]
    for n, block in enumerate(blocks):
        values, pick = block[...], pick_ref[n]
        padded = values.shape[0]
        total += weight_ref[n][:, 0:1] * dot(pick, values)
        found = dot(values[cap:padded, :padded], pick, NT)
        products += jnp.where(chosen_ref[n] > 0.5, found[0:1, :], 0.0)
    grad_ref[...] = total.astype(jnp.bfloat16)
    gate_out[...] = products.astype(jnp.bfloat16)


def combine(meta, index_rows, gate_rows, returned, early, late, cap):
    count, rows = index_rows.shape
    peers = len(early) + len(late)
    padded, share = returned[0].shape
    partial = pl.pallas_call(
        functools.partial(combine_kernel, peers, cap, early, late),
        out_shape=[
            jax.ShapeDtypeStruct((rows, share), jnp.float32),
            jax.ShapeDtypeStruct((count, rows), jnp.float32),
            jax.ShapeDtypeStruct((len(late), rows, padded), jnp.bfloat16),
            jax.ShapeDtypeStruct((len(late), rows, LANES), jnp.float32),
            jax.ShapeDtypeStruct((len(late), count, rows), jnp.float32),
        ],
        in_specs=[smem()] + [whole()] * (2 + len(early)),
        out_specs=[whole()] * 5,
        compiler_params=params(),
        cost_estimate=cost(),
        name="combine",
    )(meta, index_rows, gate_rows, *[returned[d] for d in early])
    return pl.pallas_call(
        functools.partial(combine_late_kernel, cap),
        out_shape=[
            jax.ShapeDtypeStruct((rows, share), jnp.bfloat16),
            jax.ShapeDtypeStruct((count, rows), jnp.bfloat16),
        ],
        in_specs=[whole()] * (5 + len(late)),
        out_specs=[whole()] * 2,
        compiler_params=params(),
        cost_estimate=cost(),
        name="combine_late",
    )(*partial, *[returned[d] for d in late])


def after(value, others):
    return lax.optimization_barrier((value, others))[0]


def swap_pair(block):
    count = lax.axis_size("expert")
    return lax.ppermute(block, "expert", [(i, i ^ 1) for i in range(count)])


def hidden_ring(block, r):
    count = lax.axis_size("hidden")
    return lax.ppermute(block, "hidden", [(i, (i + r) % count) for i in range(count)])


def shifted(block, d):
    count = lax.axis_size("expert")
    return lax.ppermute(block, "expert", [(i, (i + 2 * d) % count) for i in range(count)])


def chunk_groups(peers):
    rest = sorted(range(1, peers), key=lambda d: (-min(d, peers - d), d))
    rest = rest[:1] + sorted(rest[1:], key=lambda d: (min(d, peers - d), d))
    return [[0]] + [rest[n : n + 2] for n in range(0, len(rest), 2)]


def local(out_grad, expert_index, gate_values, dispatched_inputs, w_gate, w_up, w_down):
    peers = lax.axis_size("expert") // 2
    shares = lax.axis_size("hidden")
    index = lax.axis_index("expert")
    meta = jnp.stack([index // 2, index % 2, lax.axis_index("hidden")]).astype(jnp.int32)
    half_rows = dispatched_inputs.shape[1]
    cap = half_rows // peers
    sent_rows = (cap // 8 + 1) * 8
    padded = -(-sent_rows // 16) * 16
    index_rows = expert_index.T
    other_rows = swap_pair(dispatched_inputs[0])
    sent = route(meta, index_rows, out_grad, peers, sent_rows, (), shares)
    arrived = [shifted(block, d) if d else block for d, block in enumerate(sent)]

    groups = chunk_groups(peers)
    order = tuple((d, swap) for group in groups for swap in (0, 1) for d in group)
    *tables, gate_mat, up_mat, down_mat = forward(
        meta, dispatched_inputs, other_rows, w_gate, w_up, w_down, peers, cap, padded, order
    )

    gives, crossings, totals, returned = [], [], [], {}
    first = 0
    ready = {d: arrived[d] for d in groups[0]}

    def finish(n, later):
        total, parts, _ = crossings[n]
        for part in after(parts, later):
            total = total + part.astype(jnp.float32)
        totals.append(total.astype(jnp.bfloat16))
        for m, d in enumerate(groups[n]):
            block = totals[n][m * sent_rows : (m + 1) * sent_rows]
            returned[d] = shifted(block, -d) if d else block

    for n, group in enumerate(groups):
        swapped = {d: swap_pair(ready[d]) for d in group}
        cots = [[ready[d]] for d in group] + [[swapped[d]] for d in group]
        cots = after(cots, ([c[2] for c in crossings], totals, gives))
        keep, *give = backward(
            meta, cots, tables, first, gate_mat, up_mat, down_mat, cap, padded, shares
        )
        first += 2 * len(group) * padded
        gives.append(give)
        ready = {}
        for d in groups[n + 1] if n + 1 < len(groups) else []:
            ready[d] = after(arrived[d], (give, list(ready.values())))
        done = list(ready.values())
        if n:
            finish(n - 1, give)
            done.append(totals[-1])
        got = after([swap_pair(part) for part in give], done)
        pieces = [keep[r] + got[r].astype(jnp.float32) for r in range(shares)]
        crossing = [piece.astype(jnp.bfloat16) for piece in pieces[1:]]
        crossings.append((pieces[0], [hidden_ring(c, r + 1) for r, c in enumerate(crossing)], crossing))
    finish(len(groups) - 1, [])
    late = sorted({d for d in groups[1][:1] + groups[-1] if d})
    early = [d for d in range(peers) if d not in late]
    input_grad, gate_grad = combine(
        meta, index_rows, gate_values.T, returned, early, late, cap
    )
    return input_grad, gate_grad.T


def solution(mesh):
    in_specs = (
        P(("groups", "expert", "tok"), None),
        P(("groups", "expert", "tok"), None),
        P(("groups", "expert", "tok"), None),
        P("expert", ("groups", "tok"), None),
        P("expert", None, "hidden"),
        P("expert", None, "hidden"),
        P("expert", "hidden", None),
    )
    out_specs = (P(("groups", "expert", "tok"), "hidden"), P(("groups", "expert", "tok"), None))
    return jax.shard_map(local, mesh=mesh, in_specs=in_specs, out_specs=out_specs, check_vma=False)
```

```python
import functools

import jax
import jax.numpy as jnp
from jax import lax
from jax.experimental import pallas as pl
from jax.experimental.pallas import tpu as pltpu
from jax.sharding import PartitionSpec as P

LANES = 128
NT = (((1,), (1,)), ((), ()))


def params(limit=10 << 20):
    return pltpu.CompilerParams(vmem_limit_bytes=limit)


def whole():
    return pl.BlockSpec(memory_space=pltpu.VMEM)


def smem():
    return pl.BlockSpec(memory_space=pltpu.SMEM)


def cost():
    return pl.CostEstimate(flops=1000, bytes_accessed=1000, transcendentals=0)


def in_hbm(value):
    return pltpu.with_memory_space_constraint(value, pltpu.HBM)


def dot(a, b, dims=(((1,), (0,)), ((), ()))):
    return lax.dot_general(a, b, dims, preferred_element_type=jnp.float32)


def ring(value, peers):
    return jnp.where(value < 0, value + peers, value)


def named_rows(index_ref, peer, peers):
    rel = ring(index_ref[...] - peer, peers)
    count, rows = rel.shape
    expert = lax.broadcasted_iota(jnp.int32, (-(-peers // 8) * 8, rows), 0)
    named = rel[0:1, :] == expert
    for k in range(1, count):
        named = named | (rel[k : k + 1, :] == expert)
    return rel, named


def slot_rows(named):
    rows = named.shape[1]
    first = lax.broadcasted_iota(jnp.int32, (rows, rows), 0)
    second = lax.broadcasted_iota(jnp.int32, (rows, rows), 1)
    before = dot(named.astype(jnp.bfloat16), (first < second).astype(jnp.bfloat16))
    return jnp.where(named, before.astype(jnp.int32), -1)


def route_kernel(peers, padded, spread, meta, index_hbm, grad_hbm, *refs):
    outs, (index_ref, grad_ref, sems) = refs[:peers], refs[peers:]
    copies = [
        pltpu.make_async_copy(index_hbm, index_ref, sems.at[0]),
        pltpu.make_async_copy(grad_hbm, grad_ref, sems.at[1]),
    ]
    for copy in copies:
        copy.start()
    copies[0].wait()
    rows = grad_ref.shape[0]
    _, named = named_rows(index_ref, meta[0], peers)
    slots = slot_rows(named)
    place = lax.broadcasted_iota(jnp.int32, (padded, rows), 0)
    copies[1].wait()
    grad = grad_ref[...]
    for d, out in enumerate(outs):
        pick = (place == slots[d : d + 1, :]).astype(jnp.bfloat16)
        block = dot(pick, grad)
        share = out.shape[1]
        if d in spread:
            chosen = block[:, :share]
            for i in range(1, block.shape[1] // share):
                chosen = jnp.where(meta[2] == i, block[:, i * share : (i + 1) * share], chosen)
            block = chosen
        out[...] = block.astype(jnp.bfloat16)


def route(meta, index_rows, out_grad, peers, padded, spread, shares):
    width = out_grad.shape[1]
    hbm = pl.BlockSpec(memory_space=pltpu.HBM)
    return pl.pallas_call(
        functools.partial(route_kernel, peers, padded, spread),
        out_shape=[
            jax.ShapeDtypeStruct((padded, width // shares if d in spread else width), jnp.bfloat16)
            for d in range(peers)
        ],
        in_specs=[smem(), hbm, hbm],
        out_specs=[whole()] * peers,
        scratch_shapes=[
            pltpu.VMEM(index_rows.shape, index_rows.dtype),
            pltpu.VMEM(out_grad.shape, out_grad.dtype),
            pltpu.SemaphoreType.DMA((2,)),
        ],
        compiler_params=params(),
        cost_estimate=cost(),
        name="route",
    )(meta, in_hbm(index_rows), in_hbm(out_grad))


def unit_blocks(units):
    return [pl.ds(start, min(256, units - start)) for start in range(0, units, 256)]


def forward_kernel(peers, cap, padded, order, meta, own_hbm, other_ref, gate_hbm, up_hbm, down_hbm, act_ref, slope_ref, hid_ref, gate_ref, up_ref, down_ref, own_ref, rows_ref, sems):
    first = pltpu.make_async_copy(own_hbm.at[0], own_ref, sems.at[0])
    last = pltpu.make_async_copy(down_hbm.at[0], down_ref, sems.at[1])
    first.start()
    units = unit_blocks(gate_ref.shape[1])
    loads = []
    for n, unit in enumerate(units):
        loads.append(
            [
                pltpu.make_async_copy(source.at[0, :, unit], target.at[:, unit], sems.at[2 + 2 * n + m])
                for m, (source, target) in enumerate(((gate_hbm, gate_ref), (up_hbm, up_ref)))
            ]
        )
        for load in loads[-1]:
            load.start()
    last.start()
    peer, pair = meta[0], meta[1]
    first.wait()
    for values, half in ((own_ref[...], pair), (other_ref[...], 1 - pair)):
        for k in range(peers):
            source = half * peers + k
            away = ring(peer - lax.div(source, 2), peers)
            swap = jnp.where(lax.rem(source, 2) == pair, 0, 1)
            position = 0
            for n, (d, core) in enumerate(order):
                position += jnp.where((away == d) & (swap == core), n, 0)
            target = pl.ds(pl.multiple_of(position * padded, 16), padded)
            block = values[k * cap : (k + 1) * cap]
            empty = jnp.zeros((padded - cap, values.shape[1]), values.dtype)
            rows_ref[target, :] = jnp.concatenate([block, empty], axis=0)
    rows = rows_ref[...]
    for unit, load in zip(units, loads):
        for copy in load:
            copy.wait()
        gate = dot(rows, gate_ref[:, unit])
        up = dot(rows, up_ref[:, unit])
        sig = 0.5 * jnp.tanh(0.5 * gate) + 0.5
        act = gate * sig
        act_ref[:, unit] = act.astype(jnp.bfloat16)
        slope_ref[:, unit] = (up * (sig + act * (1.0 - sig))).astype(jnp.bfloat16)
        hid_ref[:, unit] = (act * up).astype(jnp.bfloat16)
    last.wait()


def forward(meta, dispatched, other, w_gate, w_up, w_down, peers, cap, padded, order):
    half_rows, width = other.shape
    units = w_gate.shape[2]
    rows = len(order) * padded
    hbm = pl.BlockSpec(memory_space=pltpu.HBM)
    weights = [w_gate, w_up, w_down]
    return pl.pallas_call(
        functools.partial(forward_kernel, peers, cap, padded, order),
        out_shape=[jax.ShapeDtypeStruct((rows, units), jnp.bfloat16)] * 3
        + [pltpu.VMEM(w.shape[1:], w.dtype) for w in weights],
        in_specs=[smem(), hbm, whole(), hbm, hbm, hbm],
        out_specs=[whole()] * 6,
        scratch_shapes=[
            pltpu.VMEM((half_rows, width), jnp.bfloat16),
            pltpu.VMEM((rows, width), jnp.bfloat16),
            pltpu.SemaphoreType.DMA((2 + 2 * len(unit_blocks(units)),)),
        ],
        compiler_params=params(14 << 20),
        cost_estimate=cost(),
        name="forward",
    )(meta, in_hbm(dispatched), other, *[in_hbm(w) for w in weights])


def backward_kernel(counts, cap, padded, first, meta, *refs):
    cots, refs = refs[: sum(counts)], refs[sum(counts) :]
    act_ref, slope_ref, hid_ref, gate_ref, up_ref, down_ref, keep = refs[:7]
    gives, (cot_ref, gate_grad, up_grad) = refs[7:-3], refs[-3:]
    sent_rows = cots[0].shape[0]
    at = 0
    for n, parts in enumerate(counts):
        pieces = [ref[...] for ref in cots[at : at + parts]]
        at += parts
        full = jnp.concatenate([pieces[-i % parts] for i in range(parts)], axis=1)
        for h in range(1, parts):
            turned = jnp.concatenate([pieces[(h - i) % parts] for i in range(parts)], axis=1)
            full = jnp.where(meta[2] == h, turned, full)
        if padded > sent_rows:
            empty = jnp.zeros((padded - sent_rows, full.shape[1]), full.dtype)
            full = jnp.concatenate([full, empty], axis=0)
        cot_ref[pl.ds(n * padded, padded), :] = full
    rows = pl.ds(first, len(counts) * padded)
    cot = cot_ref[...]
    part = jnp.zeros((len(counts) * padded, 1), jnp.float32)
    for unit in unit_blocks(gate_ref.shape[1]):
        d_hidden = dot(cot, down_ref[unit, :], NT)
        part += jnp.sum(d_hidden * hid_ref[rows, unit].astype(jnp.float32), axis=1, keepdims=True)
        gate_grad[:, unit] = (d_hidden * slope_ref[rows, unit].astype(jnp.float32)).astype(jnp.bfloat16)
        up_grad[:, unit] = (d_hidden * act_ref[rows, unit].astype(jnp.float32)).astype(jnp.bfloat16)
    back = dot(gate_grad[...], gate_ref[...], NT) + dot(up_grad[...], up_ref[...], NT)
    shares, _, share = keep.shape
    row = lax.broadcasted_iota(jnp.int32, (sent_rows, share), 0)
    lane = lax.broadcasted_iota(jnp.int32, (sent_rows, LANES), 1)
    diagonal = lax.broadcasted_iota(jnp.int32, (sent_rows, LANES), 0) == lane
    blocks = [[] for _ in range(shares)]
    for n in range(len(counts)):
        block = slice(n * padded, n * padded + sent_rows)
        line = jnp.sum(jnp.where(diagonal, part[block], 0.0), axis=0, keepdims=True)
        line = jnp.concatenate([line, jnp.zeros((1, share - LANES), jnp.float32)], axis=1)
        pieces = [back[block, i * share : (i + 1) * share] for i in range(shares)]
        for r in range(shares):
            piece = pieces[r]
            for i in range(shares):
                if i != r:
                    piece = jnp.where(meta[2] == (i - r) % shares, pieces[i], piece)
            blocks[r].append(jnp.where(row < cap, piece, jnp.where(row == cap, line, 0.0)))
    half = len(counts) // 2
    for r in range(shares):
        keep[r] = jnp.concatenate(blocks[r][:half], axis=0)
        gives[r][...] = jnp.concatenate(blocks[r][half:], axis=0).astype(jnp.bfloat16)


def backward(meta, cots, tables, first, gate_mat, up_mat, down_mat, cap, padded, shares):
    kept = len(cots) // 2 * cots[0][0].shape[0]
    width, units = gate_mat.shape
    rows = len(cots) * padded
    share = width // shares
    parts = [part for cot in cots for part in cot]
    return pl.pallas_call(
        functools.partial(backward_kernel, [len(cot) for cot in cots], cap, padded, first),
        out_shape=[
            jax.ShapeDtypeStruct((shares, kept, share), jnp.float32),
            *[jax.ShapeDtypeStruct((kept, share), jnp.bfloat16)] * shares,
        ],
        in_specs=[smem()] + [whole()] * (len(parts) + 6),
        out_specs=[whole()] * (1 + shares),
        scratch_shapes=[
            pltpu.VMEM((rows, width), jnp.bfloat16),
            pltpu.VMEM((rows, units), jnp.bfloat16),
            pltpu.VMEM((rows, units), jnp.bfloat16),
        ],
        compiler_params=params(14 << 20),
        cost_estimate=cost(),
        name="backward",
    )(meta, *parts, *tables, gate_mat, up_mat, down_mat)


def combine_kernel(peers, cap, early, late, meta, index_ref, gates_ref, *refs):
    blocks = refs[: len(early)]
    sum_ref, product_ref, pick_ref, weight_ref, chosen_ref = refs[len(early) :]
    rows, padded = sum_ref.shape[0], pick_ref.shape[2]
    rel, named = named_rows(index_ref, meta[0], peers)
    slots = slot_rows(named)
    gates = gates_ref[...]
    diagonal = lax.broadcasted_iota(jnp.int32, (rows, rows), 0) == lax.broadcasted_iota(
        jnp.int32, (rows, rows), 1
    )

    def column(row):
        return jnp.sum(jnp.where(diagonal, row, 0), axis=1, keepdims=True)

    place = lax.broadcasted_iota(jnp.int32, (rows, padded), 1)
    total = jnp.zeros(sum_ref.shape, jnp.float32)
    products = jnp.zeros(rel.shape, jnp.float32)
    for n, d in enumerate(early + late):
        chosen = rel == d
        weight = column(jnp.sum(jnp.where(chosen, gates, 0.0), axis=0, keepdims=True))
        pick = (place == column(slots[d : d + 1, :])).astype(jnp.bfloat16)
        if n < len(early):
            values = blocks[n][...]
            total += weight * dot(pick, values)
            found = dot(values[cap:padded, :padded], pick, NT)
            products += jnp.where(chosen, found[0:1, :], 0.0)
        else:
            pick_ref[n - len(early)] = pick
            weight_ref[n - len(early)] = jnp.broadcast_to(weight, weight_ref.shape[1:])
            chosen_ref[n - len(early)] = chosen.astype(jnp.float32)
    sum_ref[...] = total
    product_ref[...] = products


def combine_late_kernel(cap, sum_in, product_in, pick_ref, weight_ref, chosen_ref, *refs):
    blocks, (grad_ref, gate_out) = refs[:-2], refs[-2:]
    total = sum_in[...]
    products = product_in[...]
    for n, block in enumerate(blocks):
        values, pick = block[...], pick_ref[n]
        padded = values.shape[0]
        total += weight_ref[n][:, 0:1] * dot(pick, values)
        found = dot(values[cap:padded, :padded], pick, NT)
        products += jnp.where(chosen_ref[n] > 0.5, found[0:1, :], 0.0)
    grad_ref[...] = total.astype(jnp.bfloat16)
    gate_out[...] = products.astype(jnp.bfloat16)


def combine(meta, index_rows, gate_rows, returned, early, late, cap):
    count, rows = index_rows.shape
    peers = len(early) + len(late)
    padded, share = returned[0].shape
    partial = pl.pallas_call(
        functools.partial(combine_kernel, peers, cap, early, late),
        out_shape=[
            jax.ShapeDtypeStruct((rows, share), jnp.float32),
            jax.ShapeDtypeStruct((count, rows), jnp.float32),
            jax.ShapeDtypeStruct((len(late), rows, padded), jnp.bfloat16),
            jax.ShapeDtypeStruct((len(late), rows, LANES), jnp.float32),
            jax.ShapeDtypeStruct((len(late), count, rows), jnp.float32),
        ],
        in_specs=[smem()] + [whole()] * (2 + len(early)),
        out_specs=[whole()] * 5,
        compiler_params=params(),
        cost_estimate=cost(),
        name="combine",
    )(meta, index_rows, gate_rows, *[returned[d] for d in early])
    return pl.pallas_call(
        functools.partial(combine_late_kernel, cap),
        out_shape=[
            jax.ShapeDtypeStruct((rows, share), jnp.bfloat16),
            jax.ShapeDtypeStruct((count, rows), jnp.bfloat16),
        ],
        in_specs=[whole()] * (5 + len(late)),
        out_specs=[whole()] * 2,
        compiler_params=params(),
        cost_estimate=cost(),
        name="combine_late",
    )(*partial, *[returned[d] for d in late])


def after(value, others):
    return lax.optimization_barrier((value, others))[0]


def swap_pair(block):
    count = lax.axis_size("expert")
    return lax.ppermute(block, "expert", [(i, i ^ 1) for i in range(count)])


def hidden_ring(block, r):
    count = lax.axis_size("hidden")
    return lax.ppermute(block, "hidden", [(i, (i + r) % count) for i in range(count)])


def shifted(block, d):
    count = lax.axis_size("expert")
    return lax.ppermute(block, "expert", [(i, (i + 2 * d) % count) for i in range(count)])


def chunk_groups(peers):
    rest = sorted(range(1, peers), key=lambda d: (-min(d, peers - d), d))
    rest = rest[:1] + sorted(rest[1:], key=lambda d: (min(d, peers - d), d))
    return [[0]] + [rest[n : n + 2] for n in range(0, len(rest), 2)]


def local(out_grad, expert_index, gate_values, dispatched_inputs, w_gate, w_up, w_down):
    peers = lax.axis_size("expert") // 2
    shares = lax.axis_size("hidden")
    index = lax.axis_index("expert")
    meta = jnp.stack([index // 2, index % 2, lax.axis_index("hidden")]).astype(jnp.int32)
    half_rows = dispatched_inputs.shape[1]
    cap = half_rows // peers
    sent_rows = (cap // 8 + 1) * 8
    padded = -(-sent_rows // 16) * 16
    index_rows = expert_index.T
    other_rows = swap_pair(dispatched_inputs[0])
    sent = route(meta, index_rows, out_grad, peers, sent_rows, (), shares)
    arrived = [shifted(block, d) if d else block for d, block in enumerate(sent)]

    groups = chunk_groups(peers)
    order = tuple((d, swap) for group in groups for swap in (0, 1) for d in group)
    *tables, gate_mat, up_mat, down_mat = forward(
        meta, dispatched_inputs, other_rows, w_gate, w_up, w_down, peers, cap, padded, order
    )

    gives, crossings, totals, returned = [], [], [], {}
    first = 0
    ready = {d: arrived[d] for d in groups[0]}

    def finish(n, later):
        total, parts, _ = crossings[n]
        for part in after(parts, later):
            total = total + part.astype(jnp.float32)
        totals.append(total.astype(jnp.bfloat16))
        for m, d in enumerate(groups[n]):
            block = totals[n][m * sent_rows : (m + 1) * sent_rows]
            returned[d] = shifted(block, -d) if d else block

    for n, group in enumerate(groups):
        swapped = {d: swap_pair(ready[d]) for d in group}
        cots = [[ready[d]] for d in group] + [[swapped[d]] for d in group]
        cots = after(cots, ([c[2] for c in crossings], totals, gives))
        keep, *give = backward(
            meta, cots, tables, first, gate_mat, up_mat, down_mat, cap, padded, shares
        )
        first += 2 * len(group) * padded
        gives.append(give)
        ready = {}
        for d in groups[n + 1] if n + 1 < len(groups) else []:
            ready[d] = after(arrived[d], (give, list(ready.values())))
        done = list(ready.values())
        if n:
            finish(n - 1, give)
            done.append(totals[-1])
        got = after([swap_pair(part) for part in give], done)
        pieces = [keep[r] + got[r].astype(jnp.float32) for r in range(shares)]
        crossing = [piece.astype(jnp.bfloat16) for piece in pieces[1:]]
        crossings.append((pieces[0], [hidden_ring(c, r + 1) for r, c in enumerate(crossing)], crossing))
    finish(len(groups) - 1, [])
    late = sorted({d for d in groups[1][:1] + groups[-1] if d})
    early = [d for d in range(peers) if d not in late]
    input_grad, gate_grad = combine(
        meta, index_rows, gate_values.T, returned, early, late, cap
    )
    return input_grad, gate_grad.T


def solution(mesh):
    in_specs = (
        P(("groups", "expert", "tok"), None),
        P(("groups", "expert", "tok"), None),
        P(("groups", "expert", "tok"), None),
        P("expert", ("groups", "tok"), None),
        P("expert", None, "hidden"),
        P("expert", None, "hidden"),
        P("expert", "hidden", None),
    )
    out_specs = (P(("groups", "expert", "tok"), "hidden"), P(("groups", "expert", "tok"), None))
    return jax.shard_map(local, mesh=mesh, in_specs=in_specs, out_specs=out_specs, check_vma=False)
```
